256 devices in a mesh: expert: 32 (over x, y, core), dp: 8 (over z).
Axes of the slice: x: 4, y: 4, z: 8, core: 2. Of those that a mesh axis runs over, the one named last changes fastest.
Arguments:
- tokens: bfloat16 [8192, 2048], P(('expert', 'dp')), may hold values from -6 to 6
- upstream: bfloat16 [8192, 2048], P(('expert', 'dp')), may hold values from -4 to 4
- gate_probs: bfloat16 [8192, 8], P(('expert', 'dp')), may hold values from 0.19921875 to 1
- routes: int32 [8192, 8], P(('expert', 'dp')), may hold values from 0 to 127, all different within a row; in each aligned block of 32 rows (0 to 31, 32 to 63, ...) at most 2 rows name the same one
- w_gate: bfloat16 [256, 2048, 384], P(('expert', 'dp')), may hold values from -0.125 to 0.125
- w_up: bfloat16 [256, 2048, 384], P(('expert', 'dp')), may hold values from -0.125 to 0.125
- w_down: bfloat16 [256, 384, 2048], P(('expert', 'dp')), may hold values from -0.21875 to 0.21875
Outputs:
- input_grad: bfloat16 [8192, 2048], P(('expert', 'dp'))
- gate_prob_grad: float32 [8192, 8], P(('expert', 'dp'))
- gate_weight_grad: bfloat16 [256, 2048, 384], P(('expert', 'dp'))
- up_weight_grad: bfloat16 [256, 2048, 384], P(('expert', 'dp'))
- down_weight_grad: bfloat16 [256, 384, 2048], P(('expert', 'dp'))
The draws below stay inside these ranges and needn't reach their ends.
Inputs may be any that keep to these rules, and one draw needn't show every extreme that they name: `routes`: each row names 8 different experts. Among the rows of one device no expert is named more than 2 times, a bound that some block reaches; every expert is named somewhere.
All inputs are finite; a program needn't handle non-finite values.
Results may differ from the reference program's by a relative error of at most 0.0095.
Values may be sent and summed in bfloat16 or wider, within the bound.
A program may use at most 128 MiB of HBM per device.

```python
import math
import jax
import jax.numpy as jnp
import numpy as np
from jax import lax

D = 2048
F = 768
TOP = 8
TOK_DEV = 32
HALF = 384
EXPERTS = 128
SLOTS = 256
CAP = 2
TOKENS = 8192
N_EXPERT = 32
N_DP = 8


def block_levels(own_key, dims, cuts, least, largest):
    def one(dim, blocks):
        draws = jax.random.uniform(jax.random.fold_in(jax.random.fold_in(own_key, 6), dim), (blocks,), jnp.float32, least / len(cuts), largest / len(cuts))
        return jnp.repeat(jnp.exp(draws), dims[dim] // blocks).reshape((-1,) + (1,) * (len(dims) - dim - 1))

    factor_of = one(*cuts[0])
    for cut in cuts[1:]:
        factor_of = factor_of * one(*cut)
    return factor_of


def deal_out(own_key, own, number, rows, count, top, reach, skew):
    sequence = jax.random.permutation(own_key, count)
    crowded, ordinary = shares(count, rows * top, reach, skew, True), shares(count, rows * top, reach, skew, False)
    places = jnp.arange(count)

    def named(tallies, offset_by):
        used = int((tallies > 0).sum())
        fixed = max(1, used // 4)
        moved = fixed + (places - fixed + offset_by * (used - fixed)) % max(1, count - fixed)
        return jnp.zeros((count,), jnp.int32).at[sequence[jnp.where(places < fixed, places, moved)]].set(jnp.asarray(tallies, jnp.int32))

    tallies = jnp.where(number % 4 == 0, named(crowded, number // 4), named(ordinary, number - number // 4 - 1))
    mixed = jax.random.permutation(jax.random.fold_in(own, 3), count)
    donor, receiver = mixed[0:count // 2 * 2:2], mixed[1:count // 2 * 2:2]
    room = jnp.minimum(tallies[donor] - 1, reach - tallies[receiver]) // 2
    room = jnp.where((donor == sequence[0]) | (receiver == sequence[0]) | (tallies[receiver] == 0), 0, jnp.maximum(room, 0))
    moved = jax.random.randint(jax.random.fold_in(own, 4), (count // 2,), 0, 1 << 20) % (room + 1)
    tallies = tallies.at[donor].add(-moved).at[receiver].add(moved)
    items = jnp.searchsorted(jnp.cumsum(tallies), jnp.arange(rows * top), side="right").astype(jnp.int32)
    table = items.reshape(top, rows).T
    table = table[jax.random.permutation(jax.random.fold_in(own, 1), rows)]
    offset_by = jax.random.randint(jax.random.fold_in(own, 2), (rows, 1), 0, top)
    return jnp.take_along_axis(table, (jnp.arange(top)[None, :] + offset_by) % top, axis=1)


def shares(number_of, total, most, skew, full):
    loads = [(1 << 20) // math.isqrt(grade ** skew) + 1 for grade in range(1, number_of + 1)]
    largest = most if full else min(most, max(-(-total // number_of), total * loads[0] // sum(loads)))
    least = 1 if total - largest >= number_of - 1 else 0
    holding, spare = [largest] + [least] * (number_of - 1), total - largest - least * (number_of - 1)
    while spare > 0:
        free = [i for i in range(1, number_of) if holding[i] < largest] or [i for i in range(1, number_of) if holding[i] < most]
        pool, left = sum([loads[i] for i in free]), spare
        for i in free:
            more = min(most - holding[i], max(1, left * loads[i] // pool), spare)
            holding[i] = holding[i] + more
            spare = spare - more
    return np.array(holding)


def normal_values(rng, shape, deviation, most, pieces=(), kind=jnp.bfloat16):
    result = deviation * jax.random.normal(rng, shape, jnp.float32)
    if pieces:
        result = result * block_levels(rng, shape, pieces, -0.22, 0.18)
    return jnp.clip(result, -most, most).astype(kind)


def setup_inputs(seed: int = 0) -> dict:
    arg_keys = jax.random.split(jax.random.key(seed), 8)
    tokens = normal_values(arg_keys[0], (TOKENS, D), 1.0, 6.0, ((0, 256),))
    upstream = normal_values(arg_keys[1], (TOKENS, D), 0.25, 4.0, ((0, 256),))
    gate_probs = jnp.clip(0.19921875 + 0.80078125 * jax.random.uniform(arg_keys[2], (TOKENS, TOP), jnp.float32) ** block_levels(arg_keys[2], (TOKENS, TOP), ((0, 256),), -0.2, 0.2), 0.19921875, 1.0).astype(jnp.bfloat16)
    routes_keys = jax.random.split(jax.random.fold_in(arg_keys[3], 1), TOKENS // TOK_DEV)
    routes_turns = jax.random.permutation(jax.random.fold_in(arg_keys[3], 3), TOKENS // TOK_DEV)
    routes = jax.vmap(lambda own, number: deal_out(jax.random.fold_in(arg_keys[3], 2), own, number, TOK_DEV, EXPERTS, TOP, CAP, 2))(routes_keys, routes_turns).reshape((TOKENS, TOP))
    w_gate = normal_values(arg_keys[4], (SLOTS, D, HALF), D ** -0.5, 0.125, ((0, 256),))
    w_up = normal_values(arg_keys[5], (SLOTS, D, HALF), D ** -0.5, 0.125, ((0, 256),))
    w_down = normal_values(arg_keys[6], (SLOTS, HALF, D), F ** -0.5, 0.21875, ((0, 256),))
    return {"tokens": tokens, "upstream": upstream, "gate_probs": gate_probs, "routes": routes, "w_gate": w_gate, "w_up": w_up, "w_down": w_down}


def silu_parts(pre_gate):
    sigmoid = jax.nn.sigmoid(pre_gate)
    return pre_gate * sigmoid, sigmoid * (1.0 + pre_gate * (1.0 - sigmoid))


def reference(tokens, upstream, gate_probs, routes, w_gate, w_up, w_down):
    devices_all = N_EXPERT * N_DP
    per_device = TOK_DEV * TOP
    flat_expert = routes.reshape(devices_all, per_device).astype(jnp.int32)
    expert_range = jnp.arange(EXPERTS, dtype=jnp.int32)
    onehot = (flat_expert[:, :, None] == expert_range[None, None, :]).astype(jnp.int32)
    position = jnp.sum((jnp.cumsum(onehot, axis=1) - onehot) * onehot, axis=2).astype(jnp.int32)
    device_ids = jnp.arange(devices_all, dtype=jnp.int32)[:, None]
    route_ids = jnp.arange(per_device, dtype=jnp.int32)[None, :]
    table = jnp.full((EXPERTS, devices_all, CAP), TOKENS * TOP, jnp.int32)
    table = table.at[flat_expert, device_ids, position].set((device_ids * per_device + route_ids).astype(jnp.int32))
    zero_row = jnp.zeros((1, D), jnp.bfloat16)
    token_rows = jnp.concatenate([tokens, zero_row], axis=0)
    grad_rows = jnp.concatenate([upstream, zero_row], axis=0)
    prob_list = jnp.concatenate([gate_probs.reshape(-1), jnp.zeros((1,), jnp.bfloat16)])
    gate_split = w_gate.reshape(EXPERTS, 2, D, HALF)
    up_split = w_up.reshape(EXPERTS, 2, D, HALF)
    down_split = w_down.reshape(EXPERTS, 2, HALF, D)
    contract_rows = (((0,), (0,)), ((), ()))
    contract_cols = (((1,), (1,)), ((), ()))

    def per_expert(carried, inputs):
        input_acc, gate_acc = carried
        slot_ids, gate_pair, up_pair, down_pair = inputs
        token_ids = (slot_ids // TOP).astype(jnp.int32)
        routed_rows = token_rows[token_ids]
        routed_grads = grad_rows[token_ids]
        routed_probs = prob_list[slot_ids].astype(jnp.float32)[:, None]
        scaled = (routed_probs * routed_grads.astype(jnp.float32)).astype(jnp.bfloat16)
        gate_list = []
        up_list = []
        down_list = []
        term_list = []
        partial_list = []
        for half_index in range(2):
            gate_local = gate_pair[half_index]
            up_local = up_pair[half_index]
            down_local = down_pair[half_index]
            pre_gate = jnp.dot(routed_rows, gate_local, preferred_element_type=jnp.float32)
            pre_up = jnp.dot(routed_rows, up_local, preferred_element_type=jnp.float32)
            activation, derivative = silu_parts(pre_gate)
            hidden = (activation * pre_up).astype(jnp.bfloat16)
            back_proj = lax.dot_general(routed_grads, down_local, contract_cols, preferred_element_type=jnp.float32)
            partial_list.append(jnp.sum(hidden.astype(jnp.float32) * back_proj, axis=1))
            grad_hidden = routed_probs * back_proj
            gate_delta = (grad_hidden * pre_up * derivative).astype(jnp.bfloat16)
            up_delta = (grad_hidden * activation).astype(jnp.bfloat16)
            gate_list.append(lax.dot_general(routed_rows, gate_delta, contract_rows, preferred_element_type=jnp.float32).astype(jnp.bfloat16))
            up_list.append(lax.dot_general(routed_rows, up_delta, contract_rows, preferred_element_type=jnp.float32).astype(jnp.bfloat16))
            down_list.append(lax.dot_general(hidden, scaled, contract_rows, preferred_element_type=jnp.float32).astype(jnp.bfloat16))
            term_list.append(lax.dot_general(gate_delta, gate_local, contract_cols, preferred_element_type=jnp.float32)
                             + lax.dot_general(up_delta, up_local, contract_cols, preferred_element_type=jnp.float32))
        route_term = (term_list[0] + term_list[1]).astype(jnp.bfloat16)
        route_partial = (partial_list[0] + partial_list[1]).astype(jnp.bfloat16)
        input_acc = input_acc.at[token_ids].add(route_term.astype(jnp.float32))
        gate_acc = gate_acc.at[slot_ids].add(route_partial.astype(jnp.float32))
        outputs = (jnp.stack(gate_list), jnp.stack(up_list), jnp.stack(down_list))
        return (input_acc, gate_acc), outputs

    start = (jnp.zeros((TOKENS + 1, D), jnp.float32), jnp.zeros((TOKENS * TOP + 1,), jnp.float32))
    inputs = (table.reshape(EXPERTS, devices_all * CAP), gate_split, up_split, down_split)
    (input_acc, gate_acc), (gate_grads, up_grads, down_grads) = lax.scan(per_expert, start, inputs)
    input_grad = input_acc[:TOKENS].astype(jnp.bfloat16)
    gate_prob_grad = gate_acc[:TOKENS * TOP].reshape(TOKENS, TOP)
    return (input_grad, gate_prob_grad, gate_grads.reshape(SLOTS, D, HALF),
            up_grads.reshape(SLOTS, D, HALF), down_grads.reshape(SLOTS, HALF, D))
```

```python
import jax
import jax.numpy as jnp
from jax import lax
from jax.sharding import PartitionSpec as P


def local(tokens, upstream, gate_probs, routes, w_gate, w_up, w_down):
    columns = lax.axis_size("expert")
    rows = lax.axis_size("dp")
    token_count, width = tokens.shape
    top = routes.shape[1]
    experts = columns * rows // 2
    reach = token_count * top // experts
    per_dest = rows * reach
    pair = lax.axis_index("dp") // 2
    f32, bf16 = jnp.float32, jnp.bfloat16

    hit = routes[:, :, None] == jnp.arange(experts, dtype=jnp.int32)[None, None, :]
    named = jnp.any(hit, axis=1)
    rank = jnp.cumsum(named.astype(jnp.int32), axis=0)
    key = jnp.where(named, rank, 0).astype(bf16)
    weight = jnp.sum(jnp.where(hit, gate_probs[:, :, None].astype(f32), 0.0), axis=1).astype(bf16)
    all_tokens = lax.all_gather(tokens, "dp", axis=0, tiled=True)
    all_upstream = lax.all_gather(upstream, "dp", axis=0, tiled=True)
    info = lax.all_gather(jnp.concatenate([key, weight], axis=1), "dp", axis=0, tiled=True)
    info = info.reshape(rows * token_count, 2, columns, rows // 2)
    info = lax.dynamic_index_in_dim(info, pair, axis=3, keepdims=False)
    key_all, weight_all = info[:, 0], info[:, 1]
    source = (jnp.arange(rows * token_count) // token_count).astype(jnp.int32)
    place = jnp.where(key_all > 0, key_all.astype(jnp.int32) - 1 + reach * source[:, None], -1)
    pick = place.T[:, None, :] == jnp.arange(per_dest, dtype=jnp.int32)[None, :, None]
    pick_scaled = jnp.where(pick, weight_all.T[:, None, :], 0).astype(bf16).reshape(columns * per_dest, -1)
    pick = pick.astype(bf16).reshape(columns * per_dest, -1)
    send_rows = jnp.dot(pick, all_tokens, preferred_element_type=f32).astype(bf16)
    send_scaled = jnp.dot(pick_scaled, all_upstream, preferred_element_type=f32).astype(bf16)
    x = lax.all_to_all(send_rows, "expert", split_axis=0, concat_axis=0, tiled=True)
    scaled = lax.all_to_all(send_scaled, "expert", split_axis=0, concat_axis=0, tiled=True)

    wg, wu, wd = w_gate[0], w_up[0], w_down[0]
    over_rows = (((0,), (0,)), ((), ()))
    over_cols = (((1,), (1,)), ((), ()))
    pre_gate = jnp.dot(x, wg, preferred_element_type=f32)
    pre_up = jnp.dot(x, wu, preferred_element_type=f32)
    sigmoid = jax.nn.sigmoid(pre_gate)
    activation = pre_gate * sigmoid
    derivative = sigmoid * (1.0 + pre_gate * (1.0 - sigmoid))
    hidden = (activation * pre_up).astype(bf16)
    back = lax.dot_general(scaled, wd, over_cols, preferred_element_type=f32)
    partial = jnp.sum(hidden.astype(f32) * back, axis=1)
    gate_delta = (back * pre_up * derivative).astype(bf16)
    up_delta = (back * activation).astype(bf16)
    half_term = lax.dot_general(gate_delta, wg, over_cols, preferred_element_type=f32) + lax.dot_general(
        up_delta, wu, over_cols, preferred_element_type=f32
    )
    own_expert = lax.axis_index("expert") * (rows // 2) + pair
    marked = jnp.where(jnp.arange(experts)[None, :] == own_expert, partial[:, None], 0.0)
    back_rows = jnp.concatenate([half_term.astype(bf16), marked.astype(bf16)], axis=1)
    returned = lax.all_to_all(back_rows, "expert", split_axis=0, concat_axis=0, tiled=True)
    summed = lax.dot_general(pick, returned, over_rows, preferred_element_type=f32)
    total = lax.psum_scatter(summed, "dp", scatter_dimension=0, tiled=True)
    input_grad = total[:, :width].astype(bf16)
    route_partial = jnp.sum(jnp.where(hit, total[:, None, width:], 0.0), axis=2) / gate_probs.astype(f32)
    gate_prob_grad = route_partial.astype(bf16).astype(f32)
    gate_weight_grad = lax.dot_general(x, gate_delta, over_rows, preferred_element_type=f32).astype(bf16)[None]
    up_weight_grad = lax.dot_general(x, up_delta, over_rows, preferred_element_type=f32).astype(bf16)[None]
    down_weight_grad = lax.dot_general(hidden, scaled, over_rows, preferred_element_type=f32).astype(bf16)[None]
    return input_grad, gate_prob_grad, gate_weight_grad, up_weight_grad, down_weight_grad


def solution(mesh):
    both = ("expert", "dp")
    flat, deep = P(both, None), P(both, None, None)
    return jax.shard_map(
        local,
        mesh=mesh,
        in_specs=(flat, flat, flat, flat, deep, deep, deep),
        out_specs=(flat, flat, deep, deep, deep),
        check_vma=False,
    )
```

```python
import functools
import math

import jax
import jax.numpy as jnp
from jax import lax
from jax.experimental import pallas as pl
from jax.experimental.pallas import tpu as pltpu
from jax.sharding import PartitionSpec as P

MESH = pl.DeviceIdType.MESH
F32, BF16 = jnp.float32, jnp.bfloat16
NT = (((1,), (1,)), ((), ()))
TN = (((0,), (0,)), ((), ()))


def dot(a, b, dims=(((1,), (0,)), ((), ()))):
    return lax.dot_general(a, b, dims, preferred_element_type=F32)


def tiles(count, body):
    def step(i, carry):
        body(i)
        return carry

    lax.fori_loop(0, count, step, 0)


def kernel(sizes, *refs):
    columns, rows, tokens, width, experts, units, top, halves, returns = sizes
    (tok_hbm, ups_hbm, probs, routes, wg_hbm, wu_hbm, wd_hbm, input_grad, prob_grad, gate_out, up_out, down_out) = refs[:12]
    (ring, info, pick, pick_scaled, merge, send, recv, wgu, wd, acc, acc_back, hidden, delta, grad_gu, grad_d) = refs[12:27]
    refs = refs[27:]
    back_send, back_recv = refs[:returns], refs[returns : 2 * returns]
    row_send, row_recv = refs[2 * returns : 3 * returns], refs[3 * returns : 4 * returns]
    (own_sem, weight_sem, out_sem, ring_send_sem, ring_recv_sem, info_send_sem, info_recv_sem) = refs[4 * returns : 4 * returns + 7]
    (send_sem, recv_sem, back_send_sem, back_recv_sem, row_send_sem, row_recv_sem) = refs[4 * returns + 7 :]

    reach = tokens * top // experts
    per_dest = rows * reach
    slots = columns * per_dest
    waves = 2 * halves
    chunk = width // halves
    part = width // returns
    side = math.isqrt(columns // 2)
    me_c, me_r = lax.axis_index("expert"), lax.axis_index("dp")
    core, me_y, me_x = lax.rem(me_c, 2), lax.rem(me_c // 2, side), me_c // (2 * side)
    pair = me_r // 2

    def row_at(offset):
        return lax.rem(me_r + (offset % rows), rows)

    def column_at(i):
        dc, dy, dx = lax.rem(i, 2), lax.rem(i // 2, side), i // (2 * side)
        x, y = lax.rem(me_x + dx, side), lax.rem(me_y + dy, side)
        return (x * side + y) * 2 + lax.rem(core + dc, 2)

    def mixed(i):
        return lax.rem(i * 11, columns)

    own_copies = []
    for w in range(waves):
        source = (tok_hbm, ups_hbm)[w // halves].at[:, pl.ds((w % halves) * chunk, chunk)]
        copy = pltpu.make_async_copy(source, ring.at[w, me_r], own_sem.at[w])
        copy.start()
        own_copies.append(copy)
    weight_copies = [
        pltpu.make_async_copy(wg_hbm.at[0], wgu.at[:, pl.ds(0, units)], weight_sem.at[0]),
        pltpu.make_async_copy(wu_hbm.at[0], wgu.at[:, pl.ds(units, units)], weight_sem.at[1]),
        pltpu.make_async_copy(wd_hbm.at[0], wd, weight_sem.at[2]),
    ]
    for copy in weight_copies:
        copy.start()

    barrier = pltpu.get_barrier_semaphore()

    def greet_column(i):
        pl.semaphore_signal(barrier, inc=1, device_id=(column_at(i + 1), me_r), device_id_type=MESH)

    tiles(columns - 1, greet_column)
    for offset in range(1, rows):
        pl.semaphore_signal(barrier, inc=1, device_id=(me_c, row_at(offset)), device_id_type=MESH)

    lane = lax.broadcasted_iota(jnp.int32, (tokens, experts), 1)
    named = jnp.zeros((tokens, experts), F32)
    weight = jnp.zeros((tokens, experts), F32)
    for k in range(top):
        hit = routes[:, k : k + 1] == lane
        named = jnp.where(hit, 1.0, named)
        weight = jnp.where(hit, probs[:, k : k + 1].astype(F32), weight)
    upto = lax.broadcasted_iota(jnp.int32, (tokens, tokens), 0) >= lax.broadcasted_iota(jnp.int32, (tokens, tokens), 1)
    upto = jnp.where(upto, 1.0, 0.0).astype(BF16)
    rank = named * dot(upto, named.astype(BF16))
    info[me_r, 0:tokens, :] = rank.astype(BF16)
    info[me_r, tokens : 2 * tokens, :] = weight.astype(BF16)

    pl.semaphore_wait(barrier, columns - 1 + rows - 1)

    info_copies = []
    for offset in range(1, rows):
        copy = pltpu.make_async_remote_copy(
            info.at[me_r], info.at[me_r], info_send_sem.at[offset], info_recv_sem.at[offset],
            device_id=(me_c, row_at(offset)), device_id_type=MESH,
        )
        copy.start()
        info_copies.append(copy)

    reaches = (rows // 2, rows - 1 - rows // 2)

    def ring_copy(w, d, step):
        sign = (1 if w % 2 == 0 else -1) * (1 if d == 0 else -1)
        source = row_at(-sign * step)
        return pltpu.make_async_remote_copy(
            ring.at[w, source], ring.at[w, source], ring_send_sem.at[w, d, step], ring_recv_sem.at[w, d, step],
            device_id=(me_c, row_at(sign)), device_id_type=MESH,
        )

    def ring_arrived(w, d, step):
        sign = (1 if w % 2 == 0 else -1) * (1 if d == 0 else -1)
        source = row_at(-sign * (step + 1))
        pltpu.make_async_remote_copy(
            ring.at[w, source], ring.at[w, source], ring_send_sem.at[w, d, step], ring_recv_sem.at[w, d, step],
            device_id=(me_c, row_at(sign)), device_id_type=MESH,
        ).wait_recv()

    def make_picks():
        for offset in range(1, rows):
            source = row_at(-offset)
            pltpu.make_async_remote_copy(
                info.at[source], info.at[source], info_send_sem.at[offset], info_recv_sem.at[offset],
                device_id=(me_c, row_at(offset)), device_id_type=MESH,
            ).wait_recv()
        count = rows * tokens
        expert = lax.broadcasted_iota(jnp.int32, (experts, slots), 0)
        slot = lax.broadcasted_iota(jnp.int32, (experts, slots), 1)
        spread = jnp.where(expert == (slot // per_dest) * (rows // 2) + pair, 1.0, 0.0).astype(BF16)
        ranks = dot(info[:, 0:tokens, :].reshape(count, experts), spread)
        weights = dot(info[:, tokens : 2 * tokens, :].reshape(count, experts), spread)
        token = lax.broadcasted_iota(jnp.int32, (count, slots), 0)
        place = lax.broadcasted_iota(jnp.int32, (count, slots), 1)
        wanted = (lax.rem(place, per_dest) - reach * (token // tokens) + 1).astype(F32)
        match = (ranks > 0.5) & (ranks == wanted)
        ones = jnp.where(match, 1.0, 0.0)
        merge[...] = ones.astype(BF16)
        pick[...] = ones.T.astype(BF16)
        pick_scaled[...] = jnp.where(match, weights, 0.0).T.astype(BF16)

    step_columns = 256 if chunk % 256 == 0 else 128

    def send_wave(w):
        chosen = pick if w < halves else pick_scaled

        def one(i):
            at = pl.ds(pl.multiple_of(i * step_columns, step_columns), step_columns)
            block = ring[w, :, :, at].reshape(rows * tokens, step_columns)
            send[w, :, at] = dot(chosen[...], block).astype(BF16)

        tiles(chunk // step_columns, one)
        own = pl.ds(pl.multiple_of(me_c * per_dest, per_dest), per_dest)
        recv[w, own, :] = send[w, own, :]

        def ship(i):
            to = column_at(mixed(i + 1))
            pltpu.make_async_remote_copy(
                send.at[w, pl.ds(pl.multiple_of(to * per_dest, per_dest), per_dest)], recv.at[w, own],
                send_sem.at[w], recv_sem.at[w], device_id=(to, me_r), device_id_type=MESH,
            ).start()

        tiles(columns - 1, ship)

    for tick in range(waves + rows // 2):
        for w in range(waves):
            step = tick - w
            if step == 0:
                own_copies[w].wait()
            for d in range(2):
                if 1 <= step <= reaches[d]:
                    ring_arrived(w, d, step - 1)
                if 0 <= step < reaches[d]:
                    ring_copy(w, d, step).start()
        w = tick - rows // 2
        if w == 0:
            make_picks()
        if w >= 0:
            send_wave(w)

    for copy in weight_copies:
        copy.wait()

    others = (columns - 1) * per_dest

    def arrived(buffer, sem):
        pltpu.make_async_copy(buffer, buffer, sem).wait()

    unit_tile = 256 if (2 * units) % 256 == 0 else 128
    back_tile = 128
    for w in range(halves):
        arrived(recv.at[w, pl.ds(0, others)], recv_sem.at[w])

        def forward(i):
            at = pl.ds(pl.multiple_of(i * unit_tile, unit_tile), unit_tile)
            value = dot(recv[w], wgu[w * chunk : (w + 1) * chunk, at])
            acc[:, at] = value if w == 0 else acc[:, at] + value

        tiles(2 * units // unit_tile, forward)

    block_rows = 64

    def activate(i):
        at = pl.ds(pl.multiple_of(i * block_rows, block_rows), block_rows)
        gate, up = acc[at, 0:units], acc[at, units : 2 * units]
        sigmoid = jax.nn.sigmoid(gate)
        activation = gate * sigmoid
        hidden[at, :] = (activation * up).astype(BF16)
        acc[at, 0:units] = up * (sigmoid * (1.0 + gate * (1.0 - sigmoid)))
        acc[at, units : 2 * units] = activation

    tiles(slots // block_rows, activate)

    for w in range(halves, waves):
        arrived(recv.at[w, pl.ds(0, others)], recv_sem.at[w])
        start = (w - halves) * chunk

        def backward(i):
            at = pl.ds(pl.multiple_of(i * back_tile, back_tile), back_tile)
            value = dot(recv[w], wd[at, start : start + chunk], NT)
            acc_back[:, at] = value if w == halves else acc_back[:, at] + value

        tiles(units // back_tile, backward)

    own_expert = me_c * (rows // 2) + pair

    def deltas(i):
        at = pl.ds(pl.multiple_of(i * block_rows, block_rows), block_rows)
        back = acc_back[at, :]
        delta[at, 0:units] = (back * acc[at, 0:units]).astype(BF16)
        delta[at, units : 2 * units] = (back * acc[at, units : 2 * units]).astype(BF16)
        partial = jnp.sum(hidden[at, :].astype(F32) * back, axis=1, keepdims=True)
        place = lax.broadcasted_iota(jnp.int32, (block_rows, experts), 1)
        back_send[0][at, part : part + experts] = jnp.where(place == own_expert, partial, 0.0).astype(BF16)

    tiles(slots // block_rows, deltas)

    part_tile = 256 if part % 256 == 0 else 128
    own = pl.ds(pl.multiple_of(me_c * per_dest, per_dest), per_dest)
    for v in range(returns):

        def term(i):
            at = pl.ds(pl.multiple_of(i * part_tile, part_tile), part_tile)
            from_row = pl.ds(pl.multiple_of(v * part + i * part_tile, part_tile), part_tile)
            back_send[v][:, at] = dot(delta[...], wgu[from_row, :], NT).astype(BF16)

        tiles(part // part_tile, term)
        back_recv[v][own, :] = back_send[v][own, :]

        def ship_back(i):
            to = column_at(mixed(i + 1))
            pltpu.make_async_remote_copy(
                back_send[v].at[pl.ds(pl.multiple_of(to * per_dest, per_dest), per_dest)], back_recv[v].at[own],
                back_send_sem.at[v], back_recv_sem.at[v], device_id=(to, me_r), device_id_type=MESH,
            ).start()

        tiles(columns - 1, ship_back)

    out_copies = []
    grad_tile = 256 if chunk % 256 == 0 else 128

    def weight_gradients(w):
        def gate_up(i):
            at = pl.ds(pl.multiple_of(i * grad_tile, grad_tile), grad_tile)
            to = pl.ds(pl.multiple_of(w * chunk + i * grad_tile, grad_tile), grad_tile)
            grad_gu[to, :] = dot(recv[w, :, at], delta[...], TN).astype(BF16)

        def down(i):
            at = pl.ds(pl.multiple_of(i * grad_tile, grad_tile), grad_tile)
            to = pl.ds(pl.multiple_of(w * chunk + i * grad_tile, grad_tile), grad_tile)
            grad_d[:, to] = dot(hidden[...], recv[halves + w, :, at], TN).astype(BF16)

        tiles(chunk // grad_tile, gate_up)
        at = pl.ds(w * chunk, chunk)
        for n, out in enumerate((gate_out, up_out)):
            copy = pltpu.make_async_copy(grad_gu.at[at, pl.ds(n * units, units)], out.at[0, at, :], out_sem.at[n, w])
            copy.start()
            out_copies.append(copy)
        tiles(chunk // grad_tile, down)
        copy = pltpu.make_async_copy(grad_d.at[:, at], down_out.at[0, :, at], out_sem.at[2, w])
        copy.start()
        out_copies.append(copy)

    def combine(v):
        arrived(back_recv[v].at[pl.ds(0, others)], back_recv_sem.at[v])
        summed = dot(merge[...], back_recv[v][...]).astype(BF16).reshape(row_send[v].shape)
        row_send[v][...] = summed
        row_recv[v][me_r] = row_send[v][me_r]
        for offset in range(1, rows):
            to = row_at(offset)
            pltpu.make_async_remote_copy(
                row_send[v].at[to], row_recv[v].at[me_r], row_send_sem.at[v], row_recv_sem.at[v],
                device_id=(me_c, to), device_id_type=MESH,
            ).start()

    done = 0
    for v in range(returns):
        while done < halves and done * returns <= v * halves:
            weight_gradients(done)
            done = done + 1
        combine(v)

    for v in range(returns):
        arrived(row_recv[v].at[pl.ds(0, rows - 1)], row_recv_sem.at[v])
        total = row_recv[v][0].astype(F32)
        for r in range(1, rows):
            total = total + row_recv[v][r].astype(F32)
        input_grad[:, v * part : (v + 1) * part] = total[:, 0:part].astype(BF16)
        if v == 0:
            partials = total[:, part : part + experts]
            place = lax.broadcasted_iota(jnp.int32, (tokens, top), 1)
            result = jnp.zeros((tokens, top), F32)
            for k in range(top):
                own_value = jnp.sum(jnp.where(routes[:, k : k + 1] == lane, partials, 0.0), axis=1, keepdims=True)
                result = jnp.where(place == k, own_value, result)
            prob_grad[...] = (result / probs[...].astype(F32)).astype(BF16).astype(F32)

    for copy in info_copies:
        copy.wait_send()
    for w in range(waves):
        for d in range(2):
            for step in range(reaches[d]):
                ring_copy(w, d, step).wait_send()
        arrived(send.at[w, pl.ds(0, others)], send_sem.at[w])
    for v in range(returns):
        arrived(back_send[v].at[pl.ds(0, others)], back_send_sem.at[v])
        arrived(row_send[v].at[pl.ds(0, rows - 1)], row_send_sem.at[v])
    for copy in out_copies:
        copy.wait()


def local(halves, returns, tokens, upstream, gate_probs, routes, w_gate, w_up, w_down):
    columns, rows = lax.axis_size("expert"), lax.axis_size("dp")
    count, width = tokens.shape
    top = routes.shape[1]
    units = w_gate.shape[2]
    experts = columns * rows // 2
    per_dest = rows * (count * top // experts)
    slots = columns * per_dest
    waves, chunk, part = 2 * halves, width // halves, width // returns
    extra = [experts] + [0] * (returns - 1)
    dma = pltpu.SemaphoreType.DMA
    any_space, vmem = pl.BlockSpec(memory_space=pl.ANY), pl.BlockSpec(memory_space=pltpu.VMEM)
    return pl.pallas_call(
        functools.partial(kernel, (columns, rows, count, width, experts, units, top, halves, returns)),
        out_shape=[
            jax.ShapeDtypeStruct((count, width), BF16),
            jax.ShapeDtypeStruct((count, top), F32),
            jax.ShapeDtypeStruct(w_gate.shape, BF16),
            jax.ShapeDtypeStruct(w_up.shape, BF16),
            jax.ShapeDtypeStruct(w_down.shape, BF16),
        ],
        in_specs=[any_space, any_space, vmem, vmem, any_space, any_space, any_space],
        out_specs=[vmem, vmem, any_space, any_space, any_space],
        scratch_shapes=[
            pltpu.VMEM((waves, rows, count, chunk), BF16),
            pltpu.VMEM((rows, 2 * count, experts), BF16),
            pltpu.VMEM((slots, rows * count), BF16),
            pltpu.VMEM((slots, rows * count), BF16),
            pltpu.VMEM((rows * count, slots), BF16),
            pltpu.VMEM((waves, slots, chunk), BF16),
            pltpu.VMEM((waves, slots, chunk), BF16),
            pltpu.VMEM((width, 2 * units), BF16),
            pltpu.VMEM((units, width), BF16),
            pltpu.VMEM((slots, 2 * units), F32),
            pltpu.VMEM((slots, units), F32),
            pltpu.VMEM((slots, units), BF16),
            pltpu.VMEM((slots, 2 * units), BF16),
            pltpu.VMEM((width, 2 * units), BF16),
            pltpu.VMEM((units, width), BF16),
        ]
        + [pltpu.VMEM((slots, part + more), BF16) for more in extra] * 2
        + [pltpu.VMEM((rows, count, part + more), BF16) for more in extra] * 2
        + [
            dma((waves,)),
            dma((3,)),
            dma((3, halves)),
            dma((waves, 2, rows // 2)),
            dma((waves, 2, rows // 2)),
            dma((rows,)),
            dma((rows,)),
            dma((waves,)),
            dma((waves,)),
            dma((returns,)),
            dma((returns,)),
            dma((returns,)),
            dma((returns,)),
        ],
        compiler_params=pltpu.CompilerParams(
            collective_id=0, has_side_effects=True, vmem_limit_bytes=60 * 1024 * 1024
        ),
        cost_estimate=pl.CostEstimate(
            flops=16 * slots * width * units, bytes_accessed=24 * width * units, transcendentals=slots * units
        ),
    )(tokens, upstream, gate_probs, routes, w_gate, w_up, w_down)


def solution(mesh, halves=2, returns=4):
    both = ("expert", "dp")
    flat, deep = P(both, None), P(both, None, None)
    return jax.shard_map(
        functools.partial(local, halves, returns),
        mesh=mesh,
        in_specs=(flat, flat, flat, flat, deep, deep, deep),
        out_specs=(flat, flat, deep, deep, deep),
        check_vma=False,
    )
```

```python
import functools
import math

import jax
import jax.numpy as jnp
from jax import lax
from jax.experimental import pallas as pl
from jax.experimental.pallas import tpu as pltpu
from jax.sharding import PartitionSpec as P

MESH = pl.DeviceIdType.MESH
F32, BF16 = jnp.float32, jnp.bfloat16
NT = (((1,), (1,)), ((), ()))
TN = (((0,), (0,)), ((), ()))


def dot(a, b, dims=(((1,), (0,)), ((), ()))):
    return lax.dot_general(a, b, dims, preferred_element_type=F32)


def quotient(x, n):
    return x >> (n.bit_length() - 1) if n & (n - 1) == 0 else x // n


def remainder(x, n):
    return x & (n - 1) if n & (n - 1) == 0 else lax.rem(x, n)


def tiles(count, body):
    def step(i, carry):
        body(i)
        return carry

    lax.fori_loop(0, count, step, 0)


def kernel(sizes, plan, back_plan, *refs):
    columns, rows, tokens, width, experts, units, top = sizes
    waves, returns = len(plan), len(back_plan)
    refs = list(refs)

    def take(count):
        taken, refs[:count] = refs[:count], []
        return taken

    tok_hbm, ups_hbm, probs, routes, wg_hbm, wu_hbm, wd_hbm = take(7)
    input_grad, prob_grad, gate_out, up_out, down_out = take(5)
    info, pick, pick_scaled, merge, wgu, wd, acc, acc_back, hidden, delta, named_by = take(11)
    ring, send, recv = take(waves), take(waves), take(waves)
    back_send, back_recv, row_send, row_recv = take(returns), take(returns), take(returns), take(returns)
    own_sem, weight_sem, ring_send_sem, ring_recv_sem, info_send_sem, info_recv_sem = take(6)
    send_sem, recv_sem, swap_send_sem, swap_recv_sem = take(4)
    back_send_sem, back_recv_sem, row_send_sem, row_recv_sem = take(4)

    reach = tokens * top // experts
    per_dest = rows * reach
    slots = columns * per_dest
    half = columns // 2
    side = math.isqrt(half)
    me_c, me_r = lax.axis_index("expert"), lax.axis_index("dp")
    core, me_y, me_x = lax.rem(me_c, 2), lax.rem(me_c // 2, side), me_c // (2 * side)
    pair, parity = me_r // 2, lax.rem(me_r, 2)
    partner = me_r + 1 - 2 * parity

    def row_at(offset):
        return lax.rem(me_r + (offset % rows), rows)

    def place_at(i):
        return lax.rem(me_x + i // side, side) * side + lax.rem(me_y + lax.rem(i, side), side)

    def column_at(i):
        return place_at(i // 2) * 2 + lax.rem(core + lax.rem(i, 2), 2)

    def block(column):
        slot = lax.rem(column, 2) * half + column // 2
        return pl.ds(pl.multiple_of(slot * per_dest, per_dest), per_dest)

    def core_half(number):
        return pl.ds(pl.multiple_of(number * (half * per_dest), half * per_dest), half * per_dest)

    own = block(me_c)
    others = (columns - 1) * per_dest

    def arrived(buffer, sem):
        pltpu.make_async_copy(buffer, buffer, sem).wait()

    own_copies = []
    for w in range(waves):
        kind, start, wide = plan[w][:3]
        source = (tok_hbm, ups_hbm)[kind].at[:, pl.ds(start, wide)]
        copy = pltpu.make_async_copy(source, ring[w].at[me_r], own_sem.at[w])
        copy.start()
        own_copies.append(copy)
    weight_copies = [
        pltpu.make_async_copy(wg_hbm.at[0], wgu.at[:, pl.ds(0, units)], weight_sem.at[0]),
        pltpu.make_async_copy(wu_hbm.at[0], wgu.at[:, pl.ds(units, units)], weight_sem.at[1]),
        pltpu.make_async_copy(wd_hbm.at[0], wd, weight_sem.at[2]),
    ]
    for copy in weight_copies:
        copy.start()

    barrier = pltpu.get_barrier_semaphore()

    def greet_column(i):
        pl.semaphore_signal(barrier, inc=1, device_id=(column_at(i + 1), me_r), device_id_type=MESH)

    tiles(columns - 1, greet_column)
    for offset in range(1, rows):
        pl.semaphore_signal(barrier, inc=1, device_id=(me_c, row_at(offset)), device_id_type=MESH)

    lane = lax.broadcasted_iota(jnp.int32, (tokens, experts), 1)
    named = jnp.zeros((tokens, experts), F32)
    weight = jnp.zeros((tokens, experts), F32)
    unit = lax.broadcasted_iota(jnp.int32, (top, top), 0) == lax.broadcasted_iota(jnp.int32, (top, top), 1)
    unit = jnp.where(unit, 1.0, 0.0).astype(BF16)
    named_by[...] = dot(routes[...].astype(F32).astype(BF16), unit, TN)
    probs_by = dot(probs[...], unit, TN)
    lane = lane.astype(F32)
    for k in range(top):
        hit = named_by[:, k : k + 1] == lane
        named = jnp.where(hit, 1.0, named)
        weight = jnp.where(hit, probs_by[:, k : k + 1], weight)
    upto = lax.broadcasted_iota(jnp.int32, (tokens, tokens), 0) >= lax.broadcasted_iota(jnp.int32, (tokens, tokens), 1)
    upto = jnp.where(upto, 1.0, 0.0).astype(BF16)
    rank = named * dot(upto, named.astype(BF16))
    info[me_r, 0:tokens, :] = rank.astype(BF16)
    info[me_r, tokens : 2 * tokens, :] = weight.astype(BF16)

    pl.semaphore_wait(barrier, columns - 1 + rows - 1)

    info_copies = []
    for offset in range(1, rows):
        copy = pltpu.make_async_remote_copy(
            info.at[me_r], info.at[me_r], info_send_sem.at[offset], info_recv_sem.at[offset],
            device_id=(me_c, row_at(offset)), device_id_type=MESH,
        )
        copy.start()
        info_copies.append(copy)

    span = [k for k in range(-((rows - 1) // 2), rows // 2 + 1) if k]
    near = [k for k in span if abs(k) <= 2]
    handed = [k for k in span if abs(k) > 2]

    def gather_copy(w, offset, via):
        sign = 1 if w % 2 == 0 else -1
        source = row_at(-sign * via)
        return pltpu.make_async_remote_copy(
            ring[w].at[source], ring[w].at[source], ring_send_sem.at[w, offset % rows], ring_recv_sem.at[w, offset % rows],
            device_id=(me_c, row_at(sign * (offset - via))), device_id_type=MESH,
        )

    def gather_arrived(w, offset):
        sign = 1 if w % 2 == 0 else -1
        source = row_at(-sign * offset)
        pltpu.make_async_remote_copy(
            ring[w].at[source], ring[w].at[source], ring_send_sem.at[w, offset % rows], ring_recv_sem.at[w, offset % rows],
            device_id=(me_c, row_at(sign * offset)), device_id_type=MESH,
        ).wait_recv()

    def via_of(offset):
        return 2 if offset > 0 else -2

    def make_picks():
        for offset in range(1, rows):
            source = row_at(-offset)
            pltpu.make_async_remote_copy(
                info.at[source], info.at[source], info_send_sem.at[offset], info_recv_sem.at[offset],
                device_id=(me_c, row_at(offset)), device_id_type=MESH,
            ).wait_recv()
        count = rows * tokens
        expert = lax.broadcasted_iota(jnp.int32, (experts, slots), 0)
        slot = quotient(lax.broadcasted_iota(jnp.int32, (experts, slots), 1), per_dest)
        column = remainder(slot, half) * 2 + quotient(slot, half)
        spread = jnp.where(expert == column * (rows // 2) + pair, 1.0, 0.0).astype(BF16)
        expert = lax.broadcasted_iota(jnp.int32, (slots, experts), 1)
        slot = quotient(lax.broadcasted_iota(jnp.int32, (slots, experts), 0), per_dest)
        column = remainder(slot, half) * 2 + quotient(slot, half)
        spread_t = jnp.where(expert == column * (rows // 2) + pair, 1.0, 0.0).astype(BF16)
        ranks_in = info[:, 0:tokens, :].reshape(count, experts)
        weights_in = info[:, tokens : 2 * tokens, :].reshape(count, experts)

        def matches(ranks, token, place):
            wanted = remainder(place, per_dest) - reach * quotient(token, tokens) + 1
            return (ranks > 0.5) & (ranks == wanted.astype(F32))

        shape = (slots, count)
        match = matches(
            dot(spread_t, ranks_in, NT), lax.broadcasted_iota(jnp.int32, shape, 1), lax.broadcasted_iota(jnp.int32, shape, 0)
        )
        pick[...] = jnp.where(match, 1.0, 0.0).astype(BF16)
        pick_scaled[...] = jnp.where(match, dot(spread_t, weights_in, NT), 0.0).astype(BF16)
        shape = (count, slots)
        match = matches(
            dot(ranks_in, spread), lax.broadcasted_iota(jnp.int32, shape, 0), lax.broadcasted_iota(jnp.int32, shape, 1)
        )
        merge[...] = jnp.where(match, 1.0, 0.0).astype(BF16)

    def tile_of(wide):
        return 256 if wide % 256 == 0 else 128

    def send_wave(w):
        kind, _, wide, split = plan[w][:4]
        chosen = pick if kind == 0 else pick_scaled
        tile = tile_of(wide)

        def one(i):
            at = pl.ds(pl.multiple_of(i * tile, tile), tile)
            send[w][:, at] = dot(chosen[...], ring[w][:, :, at].reshape(rows * tokens, tile)).astype(BF16)

        tiles(wide // tile, one)

        def ship(to):
            pltpu.make_async_remote_copy(
                send[w].at[block(to)], recv[w].at[own], send_sem.at[w], recv_sem.at[w],
                device_id=(to, me_r), device_id_type=MESH,
            ).start()

        if split:
            @pl.when(parity == 0)
            def _():
                pltpu.make_async_copy(send[w].at[own], recv[w].at[own], recv_sem.at[w]).start()

            def step(i, carry):
                ship(place_at(lax.rem(i * 5, half)) * 2 + lax.rem(core + parity, 2))
                return carry

            lax.fori_loop(1 - parity, half, step, 0)
        else:
            recv[w][own, :] = send[w][own, :]
            tiles(columns - 1, lambda i: ship(column_at(lax.rem((i + 1) * 11, columns))))

    served = lax.rem(core + parity, 2)

    def swap(w):
        return pltpu.make_async_remote_copy(
            recv[w].at[core_half(served)], recv[w].at[core_half(served)], swap_send_sem.at[w], swap_recv_sem.at[w],
            device_id=(me_c, partner), device_id_type=MESH,
        )

    unit_tile = tile_of(2 * units)
    back_tile = 128
    block_rows = 64
    swapping, projected = [], []

    def project(w):
        kind, start, wide = plan[w][:3]
        opens = all(plan[v][0] != kind for v in projected)

        def forward(i):
            at = pl.ds(pl.multiple_of(i * unit_tile, unit_tile), unit_tile)
            value = dot(recv[w][...], wgu[start : start + wide, at])
            acc[:, at] = value if opens else acc[:, at] + value

        def backward(i):
            at = pl.ds(pl.multiple_of(i * back_tile, back_tile), back_tile)
            value = dot(recv[w][...], wd[at, start : start + wide], NT)
            acc_back[:, at] = value if opens else acc_back[:, at] + value

        if kind == 0:
            tiles(2 * units // unit_tile, forward)
        else:
            tiles(units // back_tile, backward)

    def activate(i):
        at = pl.ds(pl.multiple_of(i * block_rows, block_rows), block_rows)
        gate, up = acc[at, 0:units], acc[at, units : 2 * units]
        sigmoid = jax.nn.sigmoid(gate)
        activation = gate * sigmoid
        hidden[at, :] = (activation * up).astype(BF16)
        acc[at, 0:units] = up * (sigmoid * (1.0 + gate * (1.0 - sigmoid)))
        acc[at, units : 2 * units] = activation

    def finish(w):
        if plan[w][3]:
            swap(w).wait_recv()
        project(w)
        projected.append(w)
        if plan[w][0] == 0 and all(v in projected for v in range(waves) if plan[v][0] == 0):
            tiles(slots // block_rows, activate)

    direct = [not handed or steps == 1 for *_, steps in plan]
    started = [max(0, w - lead) for w, (*_, lead, _) in enumerate(plan)]
    relayed = [min(w, started[w] + 1) for w in range(waves)]
    farthest = sorted(span, key=lambda k: -abs(k))
    for tick in range(waves + PACE):
        for w in range(waves):
            if tick == started[w]:
                own_copies[w].wait()
                for offset in farthest if direct[w] else sorted(near, key=lambda k: -abs(k)):
                    gather_copy(w, offset, 0).start()
        if tick == 0:
            make_picks()
        for w in range(waves):
            if tick == relayed[w] and not direct[w]:
                for via in sorted(set(via_of(offset) for offset in handed)):
                    gather_arrived(w, via)
                    for offset in handed:
                        if via_of(offset) == via:
                            gather_copy(w, offset, via).start()
        if tick < waves:
            for offset in span:
                if direct[tick] or offset in handed or all(via_of(other) != offset for other in handed):
                    gather_arrived(tick, offset)
        landed = tick - PACE
        if landed == 0:
            for copy in weight_copies:
                copy.wait()
        if landed >= 0:
            if plan[landed][3]:
                arrived(recv[landed].at[core_half(served)], recv_sem.at[landed])
                swap(landed).start()
                swapping.append(landed)
            else:
                arrived(recv[landed].at[pl.ds(0, others)], recv_sem.at[landed])
        if tick < waves:
            send_wave(tick)
        if landed >= 0 and not plan[landed][3]:
            finish(landed)
        while swapping and (swapping[0] <= landed - SWAP_LAG or landed == waves - 1):
            finish(swapping.pop(0))

    own_expert = me_c * (rows // 2) + pair

    def deltas(i):
        at = pl.ds(pl.multiple_of(i * block_rows, block_rows), block_rows)
        back = acc_back[at, :]
        delta[at, 0:units] = (back * acc[at, 0:units]).astype(BF16)
        delta[at, units : 2 * units] = (back * acc[at, units : 2 * units]).astype(BF16)
        partial = jnp.sum(hidden[at, :].astype(F32) * back, axis=1, keepdims=True)
        place = lax.broadcasted_iota(jnp.int32, (block_rows, experts), 1)
        mark = back_plan[MARKED][1]
        back_send[MARKED][at, mark : mark + experts] = jnp.where(place == own_expert, partial, 0.0).astype(BF16)

    tiles(slots // block_rows, deltas)

    def send_back(v):
        start, wide = back_plan[v]
        part_tile = tile_of(wide)

        def term(i):
            at = pl.ds(pl.multiple_of(i * part_tile, part_tile), part_tile)
            from_row = pl.ds(pl.multiple_of(start + i * part_tile, part_tile), part_tile)
            back_send[v][:, at] = dot(delta[...], wgu[from_row, :], NT).astype(BF16)

        tiles(wide // part_tile, term)
        back_recv[v][own, :] = back_send[v][own, :]

        def ship_back(i):
            to = column_at(lax.rem((i + 1) * 11, columns))
            pltpu.make_async_remote_copy(
                back_send[v].at[block(to)], back_recv[v].at[own], back_send_sem.at[v], back_recv_sem.at[v],
                device_id=(to, me_r), device_id_type=MESH,
            ).start()

        tiles(columns - 1, ship_back)

    def weight_gradients(w):
        kind, start, wide = plan[w][:3]
        tile = tile_of(wide)

        def gate_up(i):
            at = pl.ds(pl.multiple_of(i * tile, tile), tile)
            to = pl.ds(pl.multiple_of(start + i * tile, tile), tile)
            value = dot(recv[w][:, at], delta[...], TN).astype(BF16)
            gate_out[0, to, :] = value[:, 0:units]
            up_out[0, to, :] = value[:, units : 2 * units]

        def down(i):
            at = pl.ds(pl.multiple_of(i * tile, tile), tile)
            to = pl.ds(pl.multiple_of(start + i * tile, tile), tile)
            down_out[0, :, to] = dot(hidden[...], recv[w][:, at], TN).astype(BF16)

        tiles(wide // tile, gate_up if kind == 0 else down)

    def combine(v):
        arrived(back_recv[v].at[pl.ds(0, others)], back_recv_sem.at[v])
        summed = dot(merge[...], back_recv[v][...]).astype(BF16).reshape(row_send[v].shape)
        row_send[v][...] = summed
        row_recv[v][me_r] = row_send[v][me_r]
        for offset in range(1, rows):
            to = row_at(offset)
            pltpu.make_async_remote_copy(
                row_send[v].at[to], row_recv[v].at[me_r], row_send_sem.at[v], row_recv_sem.at[v],
                device_id=(me_c, to), device_id_type=MESH,
            ).start()

    done = 0
    for v in range(min(WINDOW, returns)):
        send_back(v)
    for v in range(returns):
        while done < waves and done * returns <= (v + 1) * waves:
            weight_gradients(done)
            done = done + 1
        combine(v)
        if v + WINDOW < returns:
            send_back(v + WINDOW)

    for v in range(returns):
        start, wide = back_plan[v]
        arrived(row_recv[v].at[pl.ds(0, rows - 1)], row_recv_sem.at[v])
        total = row_recv[v][0].astype(F32)
        for r in range(1, rows):
            total = total + row_recv[v][r].astype(F32)
        input_grad[:, start : start + wide] = total[:, 0:wide].astype(BF16)
        if v == MARKED:
            partials = total[:, wide : wide + experts]
            place = lax.broadcasted_iota(jnp.int32, (tokens, top), 1)
            result = jnp.zeros((tokens, top), F32)
            for k in range(top):
                own_value = jnp.sum(jnp.where(named_by[:, k : k + 1] == lane, partials, 0.0), axis=1, keepdims=True)
                result = jnp.where(place == k, own_value / probs_by[:, k : k + 1], result)
            token_unit = lax.broadcasted_iota(jnp.int32, (tokens, tokens), 0) == lax.broadcasted_iota(jnp.int32, (tokens, tokens), 1)
            prob_grad[...] = dot(result.astype(BF16), jnp.where(token_unit, 1.0, 0.0).astype(BF16), TN)

    for copy in info_copies:
        copy.wait_send()
    for w in range(waves):
        for offset in span:
            gather_copy(w, offset, via_of(offset) if offset in handed and not direct[w] else 0).wait_send()
        if plan[w][3]:
            swap(w).wait_send()
            served_rows = (half - 1) * per_dest
            if served_rows:
                arrived(send[w].at[pl.ds(0, served_rows)], send_sem.at[w])

            @pl.when(parity == 1)
            def _():
                arrived(send[w].at[pl.ds(0, per_dest)], send_sem.at[w])
        else:
            arrived(send[w].at[pl.ds(0, others)], send_sem.at[w])
    for v in range(returns):
        arrived(back_send[v].at[pl.ds(0, others)], back_send_sem.at[v])
        arrived(row_send[v].at[pl.ds(0, rows - 1)], row_send_sem.at[v])


def local(plan, back_plan, tokens, upstream, gate_probs, routes, w_gate, w_up, w_down):
    columns, rows = lax.axis_size("expert"), lax.axis_size("dp")
    count, width = tokens.shape
    top = routes.shape[1]
    units = w_gate.shape[2]
    experts = columns * rows // 2
    slots = columns * rows * (count * top // experts)
    waves, returns = len(plan), len(back_plan)
    wides = [wave[2] for wave in plan]
    backs = [wide + (experts if v == MARKED else 0) for v, (_, wide) in enumerate(back_plan)]
    dma = pltpu.SemaphoreType.DMA
    any_space, vmem = pl.BlockSpec(memory_space=pl.ANY), pl.BlockSpec(memory_space=pltpu.VMEM)
    input_grad, prob_grad, gate_grad, up_grad, down_grad = pl.pallas_call(
        functools.partial(kernel, (columns, rows, count, width, experts, units, top), plan, back_plan),
        out_shape=[
            pltpu.VMEM((count, width), BF16),
            pltpu.VMEM((top, count), F32),
            pltpu.VMEM(w_gate.shape, BF16),
            pltpu.VMEM(w_up.shape, BF16),
            pltpu.VMEM(w_down.shape, BF16),
        ],
        in_specs=[any_space, any_space, vmem, vmem, any_space, any_space, any_space],
        out_specs=[vmem] * 5,
        scratch_shapes=[
            pltpu.VMEM((rows, 2 * count, experts), BF16),
            pltpu.VMEM((slots, rows * count), BF16),
            pltpu.VMEM((slots, rows * count), BF16),
            pltpu.VMEM((rows * count, slots), BF16),
            pltpu.VMEM((width, 2 * units), BF16),
            pltpu.VMEM((units, width), BF16),
            pltpu.VMEM((slots, 2 * units), F32),
            pltpu.VMEM((slots, units), F32),
            pltpu.VMEM((slots, units), BF16),
            pltpu.VMEM((slots, 2 * units), BF16),
            pltpu.VMEM((count, top), F32),
        ]
        + [pltpu.VMEM((rows, count, wide), BF16) for wide in wides]
        + [pltpu.VMEM((slots, wide), BF16) for wide in wides] * 2
        + [pltpu.VMEM((slots, wide), BF16) for wide in backs] * 2
        + [pltpu.VMEM((rows, count, wide), BF16) for wide in backs] * 2
        + [
            dma((waves,)),
            dma((3,)),
            dma((waves, rows)),
            dma((waves, rows)),
            dma((rows,)),
            dma((rows,)),
            dma((waves,)),
            dma((waves,)),
            dma((waves,)),
            dma((waves,)),
            dma((returns,)),
            dma((returns,)),
            dma((returns,)),
            dma((returns,)),
        ],
        compiler_params=pltpu.CompilerParams(
            collective_id=0, has_side_effects=True, vmem_limit_bytes=48 * 1024 * 1024
        ),
        cost_estimate=pl.CostEstimate(
            flops=16 * slots * width * units, bytes_accessed=24 * width * units, transcendentals=slots * units
        ),
    )(tokens, upstream, gate_probs.T, routes.T, w_gate, w_up, w_down)
    return input_grad, prob_grad.T, gate_grad, up_grad, down_grad


PLAN = (
    (0, 0, 1, 0, 4, 1),
    (0, 1, 1, 0, 4, 2),
    (0, 2, 2, 1, 4, 2),
    (0, 4, 2, 1, 4, 2),
    (0, 6, 2, 1, 4, 2),
    (1, 0, 2, 1, 4, 2),
    (1, 2, 2, 0, 4, 2),
    (1, 4, 2, 0, 4, 2),
    (1, 6, 2, 0, 4, 2),
)
PACE, SWAP_LAG = 3, 2
BACK_PLAN = ((0, 1), (1, 1), (2, 2), (4, 2), (6, 1), (7, 1))
MARKED = 1
WINDOW = 3


def solution(mesh):
    both = ("expert", "dp")
    flat, deep = P(both, None), P(both, None, None)

    def whole(tokens, *others):
        unit = tokens.shape[1] // 8
        plan = tuple((kind, start * unit, wide * unit, bool(split), *rest) for kind, start, wide, split, *rest in PLAN)
        back_plan = tuple((start * unit, wide * unit) for start, wide in BACK_PLAN)
        return jax.shard_map(
            functools.partial(local, plan, back_plan),
            mesh=mesh,
            in_specs=(flat, flat, flat, flat, deep, deep, deep),
            out_specs=(flat, flat, deep, deep, deep),
            check_vma=False,
        )(tokens, *others)

    return whole
```

```python
import functools
import math

import jax
import jax.numpy as jnp
from jax import lax
from jax.experimental import pallas as pl
from jax.experimental.pallas import tpu as pltpu
from jax.sharding import PartitionSpec as P

MESH = pl.DeviceIdType.MESH
F32, BF16 = jnp.float32, jnp.bfloat16
NT = (((1,), (1,)), ((), ()))
TN = (((0,), (0,)), ((), ()))


def dot(a, b, dims=(((1,), (0,)), ((), ()))):
    return lax.dot_general(a, b, dims, preferred_element_type=F32)


def quotient(x, n):
    return x >> (n.bit_length() - 1) if n & (n - 1) == 0 else x // n


def remainder(x, n):
    return x & (n - 1) if n & (n - 1) == 0 else lax.rem(x, n)


def tiles(count, body):
    def step(i, carry):
        body(i)
        return carry

    lax.fori_loop(0, count, step, 0)


def kernel(sizes, plan, back_plan, *refs):
    columns, rows, tokens, width, experts, units, top = sizes
    waves, returns = len(plan), len(back_plan)
    refs = list(refs)

    def take(count):
        taken, refs[:count] = refs[:count], []
        return taken

    tok_hbm, ups_hbm, probs_hbm, routes_hbm, wg_hbm, wu_hbm, wd_hbm = take(7)
    input_grad, prob_grad, gate_out, up_out, down_out = take(5)
    info, pick, pick_scaled, merge, wgu, wd, acc, acc_back, hidden, delta, named_by, probs, routes = take(13)
    ring, send, recv = take(waves), take(waves), take(waves)
    back_send, back_recv, row_send, row_recv = take(returns), take(returns), take(returns), take(returns)
    own_sem, weight_sem, ring_send_sem, ring_recv_sem, info_send_sem, info_recv_sem = take(6)
    send_sem, recv_sem, swap_send_sem, swap_recv_sem = take(4)
    back_send_sem, back_recv_sem, row_send_sem, row_recv_sem = take(4)

    reach = tokens * top // experts
    per_dest = rows * reach
    slots = columns * per_dest
    half = columns // 2
    side = math.isqrt(half)
    me_c, me_r = lax.axis_index("expert"), lax.axis_index("dp")
    core, me_y, me_x = lax.rem(me_c, 2), lax.rem(me_c // 2, side), me_c // (2 * side)
    pair, parity = me_r // 2, lax.rem(me_r, 2)
    partner = me_r + 1 - 2 * parity

    def row_at(offset):
        return lax.rem(me_r + (offset % rows), rows)

    def place_at(i):
        return lax.rem(me_x + i // side, side) * side + lax.rem(me_y + lax.rem(i, side), side)

    def column_at(i):
        return place_at(i // 2) * 2 + lax.rem(core + lax.rem(i, 2), 2)

    def block(column):
        slot = lax.rem(column, 2) * half + column // 2
        return pl.ds(pl.multiple_of(slot * per_dest, per_dest), per_dest)

    def core_half(number):
        return pl.ds(pl.multiple_of(number * (half * per_dest), half * per_dest), half * per_dest)

    own = block(me_c)
    others = (columns - 1) * per_dest

    def arrived(buffer, sem):
        pltpu.make_async_copy(buffer, buffer, sem).wait()

    own_copies = []
    for w in range(waves):
        kind, start, wide = plan[w][:3]
        source = (tok_hbm, ups_hbm)[kind].at[:, pl.ds(start, wide)]
        copy = pltpu.make_async_copy(source, ring[w].at[me_r], own_sem.at[w])
        copy.start()
        own_copies.append(copy)
    route_copies = [
        pltpu.make_async_copy(probs_hbm, probs, weight_sem.at[3]),
        pltpu.make_async_copy(routes_hbm, routes, weight_sem.at[4]),
    ]
    for copy in route_copies:
        copy.start()
    weight_copies = [
        pltpu.make_async_copy(wg_hbm.at[0], wgu.at[:, pl.ds(0, units)], weight_sem.at[0]),
        pltpu.make_async_copy(wu_hbm.at[0], wgu.at[:, pl.ds(units, units)], weight_sem.at[1]),
        pltpu.make_async_copy(wd_hbm.at[0], wd, weight_sem.at[2]),
    ]
    for copy in weight_copies:
        copy.start()

    barrier = pltpu.get_barrier_semaphore()

    def greet_column(i):
        pl.semaphore_signal(barrier, inc=1, device_id=(column_at(i + 1), me_r), device_id_type=MESH)

    tiles(columns - 1, greet_column)
    for offset in range(1, rows):
        pl.semaphore_signal(barrier, inc=1, device_id=(me_c, row_at(offset)), device_id_type=MESH)

    for copy in route_copies:
        copy.wait()

    lane = lax.broadcasted_iota(jnp.int32, (tokens, experts), 1)
    named = jnp.zeros((tokens, experts), F32)
    weight = jnp.zeros((tokens, experts), F32)
    unit = lax.broadcasted_iota(jnp.int32, (top, top), 0) == lax.broadcasted_iota(jnp.int32, (top, top), 1)
    unit = jnp.where(unit, 1.0, 0.0).astype(BF16)
    named_by[...] = dot(routes[...].astype(F32).astype(BF16), unit, TN)
    probs_by = dot(probs[...], unit, TN)
    lane = lane.astype(F32)
    for k in range(top):
        hit = named_by[:, k : k + 1] == lane
        named = jnp.where(hit, 1.0, named)
        weight = jnp.where(hit, probs_by[:, k : k + 1], weight)
    upto = lax.broadcasted_iota(jnp.int32, (tokens, tokens), 0) >= lax.broadcasted_iota(jnp.int32, (tokens, tokens), 1)
    upto = jnp.where(upto, 1.0, 0.0).astype(BF16)
    rank = named * dot(upto, named.astype(BF16))
    info[me_r, 0:tokens, :] = rank.astype(BF16)
    info[me_r, tokens : 2 * tokens, :] = weight.astype(BF16)

    pl.semaphore_wait(barrier, columns - 1 + rows - 1)

    info_copies = []
    for offset in range(1, rows):
        copy = pltpu.make_async_remote_copy(
            info.at[me_r], info.at[me_r], info_send_sem.at[offset], info_recv_sem.at[offset],
            device_id=(me_c, row_at(offset)), device_id_type=MESH,
        )
        copy.start()
        info_copies.append(copy)

    span = [k for k in range(-((rows - 1) // 2), rows // 2 + 1) if k]

    def via_of(w, offset):
        steps, way = plan[w][5], 1 if offset > 0 else -1
        if steps == 1 or abs(offset) <= (2 if steps == 2 else 1):
            return 0
        return 2 * way if steps == 2 else offset - way

    def stage_of(w, offset):
        via = via_of(w, offset)
        return 0 if via == 0 else stage_of(w, via) + 1

    def gather_copy(w, offset, via):
        sign = 1 if w % 2 == 0 else -1
        source = row_at(-sign * via)
        return pltpu.make_async_remote_copy(
            ring[w].at[source], ring[w].at[source], ring_send_sem.at[w, offset % rows], ring_recv_sem.at[w, offset % rows],
            device_id=(me_c, row_at(sign * (offset - via))), device_id_type=MESH,
        )

    def gather_arrived(w, offset):
        sign = 1 if w % 2 == 0 else -1
        source = row_at(-sign * offset)
        pltpu.make_async_remote_copy(
            ring[w].at[source], ring[w].at[source], ring_send_sem.at[w, offset % rows], ring_recv_sem.at[w, offset % rows],
            device_id=(me_c, row_at(sign * offset)), device_id_type=MESH,
        ).wait_recv()

    def make_picks():
        for offset in range(1, rows):
            source = row_at(-offset)
            pltpu.make_async_remote_copy(
                info.at[source], info.at[source], info_send_sem.at[offset], info_recv_sem.at[offset],
                device_id=(me_c, row_at(offset)), device_id_type=MESH,
            ).wait_recv()
        count = rows * tokens
        expert = lax.broadcasted_iota(jnp.int32, (experts, slots), 0)
        slot = quotient(lax.broadcasted_iota(jnp.int32, (experts, slots), 1), per_dest)
        column = remainder(slot, half) * 2 + quotient(slot, half)
        spread = jnp.where(expert == column * (rows // 2) + pair, 1.0, 0.0).astype(BF16)
        expert = lax.broadcasted_iota(jnp.int32, (slots, experts), 1)
        slot = quotient(lax.broadcasted_iota(jnp.int32, (slots, experts), 0), per_dest)
        column = remainder(slot, half) * 2 + quotient(slot, half)
        spread_t = jnp.where(expert == column * (rows // 2) + pair, 1.0, 0.0).astype(BF16)
        ranks_in = info[:, 0:tokens, :].reshape(count, experts)
        weights_in = info[:, tokens : 2 * tokens, :].reshape(count, experts)

        def matches(ranks, token, place):
            wanted = remainder(place, per_dest) - reach * quotient(token, tokens) + 1
            return (ranks > 0.5) & (ranks == wanted.astype(F32))

        shape = (slots, count)
        match = matches(
            dot(spread_t, ranks_in, NT), lax.broadcasted_iota(jnp.int32, shape, 1), lax.broadcasted_iota(jnp.int32, shape, 0)
        )
        pick[...] = jnp.where(match, 1.0, 0.0).astype(BF16)
        pick_scaled[...] = jnp.where(match, dot(spread_t, weights_in, NT), 0.0).astype(BF16)
        shape = (count, slots)
        match = matches(
            dot(ranks_in, spread), lax.broadcasted_iota(jnp.int32, shape, 0), lax.broadcasted_iota(jnp.int32, shape, 1)
        )
        merge[...] = jnp.where(match, 1.0, 0.0).astype(BF16)

    def tile_of(wide):
        return 256 if wide % 256 == 0 else 128

    def send_wave(w):
        kind, _, wide, split = plan[w][:4]
        chosen = pick if kind == 0 else pick_scaled
        tile = tile_of(wide)

        def one(i):
            at = pl.ds(pl.multiple_of(i * tile, tile), tile)
            send[w][:, at] = dot(chosen[...], ring[w][:, :, at].reshape(rows * tokens, tile)).astype(BF16)

        tiles(wide // tile, one)

        def ship(to):
            pltpu.make_async_remote_copy(
                send[w].at[block(to)], recv[w].at[own], send_sem.at[w], recv_sem.at[w],
                device_id=(to, me_r), device_id_type=MESH,
            ).start()

        if split:
            @pl.when(parity == 0)
            def _():
                pltpu.make_async_copy(send[w].at[own], recv[w].at[own], recv_sem.at[w]).start()

            def step(i, carry):
                ship(place_at(lax.rem(i * 5, half)) * 2 + lax.rem(core + parity, 2))
                return carry

            lax.fori_loop(1 - parity, half, step, 0)
        else:
            recv[w][own, :] = send[w][own, :]
            tiles(columns - 1, lambda i: ship(column_at(lax.rem((i + 1) * 11, columns))))

    served = lax.rem(core + parity, 2)

    def swap(w):
        return pltpu.make_async_remote_copy(
            recv[w].at[core_half(served)], recv[w].at[core_half(served)], swap_send_sem.at[w], swap_recv_sem.at[w],
            device_id=(me_c, partner), device_id_type=MESH,
        )

    unit_tile = tile_of(2 * units)
    back_tile = 128
    block_rows = 64
    swapping, projected = [], []

    def project(w):
        kind, start, wide = plan[w][:3]
        opens = all(plan[v][0] != kind for v in projected)

        def forward(i):
            at = pl.ds(pl.multiple_of(i * unit_tile, unit_tile), unit_tile)
            value = dot(recv[w][...], wgu[start : start + wide, at])
            acc[:, at] = value if opens else acc[:, at] + value

        def backward(i):
            at = pl.ds(pl.multiple_of(i * back_tile, back_tile), back_tile)
            value = dot(recv[w][...], wd[at, start : start + wide], NT)
            acc_back[:, at] = value if opens else acc_back[:, at] + value

        if kind == 0:
            tiles(2 * units // unit_tile, forward)
        else:
            tiles(units // back_tile, backward)

    def activate(i):
        at = pl.ds(pl.multiple_of(i * block_rows, block_rows), block_rows)
        gate, up = acc[at, 0:units], acc[at, units : 2 * units]
        sigmoid = jax.nn.sigmoid(gate)
        activation = gate * sigmoid
        hidden[at, :] = (activation * up).astype(BF16)
        acc[at, 0:units] = up * (sigmoid * (1.0 + gate * (1.0 - sigmoid)))
        acc[at, units : 2 * units] = activation

    def finish(w):
        if plan[w][3]:
            swap(w).wait_recv()
        project(w)
        projected.append(w)
        if plan[w][0] == 0 and all(v in projected for v in range(waves) if plan[v][0] == 0):
            tiles(slots // block_rows, activate)

    started = [start for *_, start, _ in plan]
    heard = set()

    def hear(w, offset):
        if (w, offset) not in heard:
            heard.add((w, offset))
            gather_arrived(w, offset)

    farthest = sorted(span, key=lambda k: -abs(k))
    for tick in range(waves + PACE):
        for w in range(waves):
            for stage in range(rows):
                if tick != min(w, started[w] + stage):
                    continue
                if stage == 0:
                    own_copies[w].wait()
                for offset in farthest:
                    if stage_of(w, offset) == stage:
                        via = via_of(w, offset)
                        if via:
                            hear(w, via)
                        gather_copy(w, offset, via).start()
        if tick == 0:
            make_picks()
        if tick < waves:
            for offset in span:
                hear(tick, offset)
        landed = tick - PACE
        if landed == 0:
            for copy in weight_copies:
                copy.wait()
        if landed >= 0:
            if plan[landed][3]:
                arrived(recv[landed].at[core_half(served)], recv_sem.at[landed])
                swap(landed).start()
                swapping.append(landed)
            else:
                arrived(recv[landed].at[pl.ds(0, others)], recv_sem.at[landed])
        if tick < waves:
            send_wave(tick)
        if landed >= 0 and not plan[landed][3]:
            finish(landed)
        while swapping and (swapping[0] <= landed - SWAP_LAG or landed == waves - 1):
            finish(swapping.pop(0))

    own_expert = me_c * (rows // 2) + pair

    def deltas(i):
        at = pl.ds(pl.multiple_of(i * block_rows, block_rows), block_rows)
        back = acc_back[at, :]
        delta[at, 0:units] = (back * acc[at, 0:units]).astype(BF16)
        delta[at, units : 2 * units] = (back * acc[at, units : 2 * units]).astype(BF16)
        partial = jnp.sum(hidden[at, :].astype(F32) * back, axis=1, keepdims=True)
        place = lax.broadcasted_iota(jnp.int32, (block_rows, experts), 1)
        mark = back_plan[MARKED][1]
        back_send[MARKED][at, mark : mark + experts] = jnp.where(place == own_expert, partial, 0.0).astype(BF16)

    tiles(slots // block_rows, deltas)

    def send_back(v):
        start, wide = back_plan[v]
        part_tile = tile_of(wide)

        def term(i):
            at = pl.ds(pl.multiple_of(i * part_tile, part_tile), part_tile)
            from_row = pl.ds(pl.multiple_of(start + i * part_tile, part_tile), part_tile)
            back_send[v][:, at] = dot(delta[...], wgu[from_row, :], NT).astype(BF16)

        tiles(wide // part_tile, term)
        back_recv[v][own, :] = back_send[v][own, :]

        def ship_back(i):
            to = column_at(lax.rem((i + 1) * 11, columns))
            pltpu.make_async_remote_copy(
                back_send[v].at[block(to)], back_recv[v].at[own], back_send_sem.at[v], back_recv_sem.at[v],
                device_id=(to, me_r), device_id_type=MESH,
            ).start()

        tiles(columns - 1, ship_back)

    def weight_gradients(w):
        kind, start, wide = plan[w][:3]
        tile = tile_of(wide)

        def gate_up(i):
            at = pl.ds(pl.multiple_of(i * tile, tile), tile)
            to = pl.ds(pl.multiple_of(start + i * tile, tile), tile)
            value = dot(recv[w][:, at], delta[...], TN).astype(BF16)
            gate_out[0, to, :] = value[:, 0:units]
            up_out[0, to, :] = value[:, units : 2 * units]

        def down(i):
            at = pl.ds(pl.multiple_of(i * tile, tile), tile)
            to = pl.ds(pl.multiple_of(start + i * tile, tile), tile)
            down_out[0, :, to] = dot(hidden[...], recv[w][:, at], TN).astype(BF16)

        tiles(wide // tile, gate_up if kind == 0 else down)

    def combine(v):
        arrived(back_recv[v].at[pl.ds(0, others)], back_recv_sem.at[v])
        summed = dot(merge[...], back_recv[v][...]).astype(BF16).reshape(row_send[v].shape)
        row_send[v][...] = summed
        row_recv[v][me_r] = row_send[v][me_r]
        for offset in range(1, rows):
            to = row_at(offset)
            pltpu.make_async_remote_copy(
                row_send[v].at[to], row_recv[v].at[me_r], row_send_sem.at[v], row_recv_sem.at[v],
                device_id=(me_c, to), device_id_type=MESH,
            ).start()

    done = 0
    for v in range(min(WINDOW, returns)):
        send_back(v)
    for v in range(returns):
        while done < waves and done * returns <= (v + 1) * waves:
            weight_gradients(done)
            done = done + 1
        combine(v)
        if v + WINDOW < returns:
            send_back(v + WINDOW)

    for v in range(returns):
        start, wide = back_plan[v]
        arrived(row_recv[v].at[pl.ds(0, rows - 1)], row_recv_sem.at[v])
        total = row_recv[v][0].astype(F32)
        for r in range(1, rows):
            total = total + row_recv[v][r].astype(F32)
        input_grad[:, start : start + wide] = total[:, 0:wide].astype(BF16)
        if v == MARKED:
            partials = total[:, wide : wide + experts]
            place = lax.broadcasted_iota(jnp.int32, (tokens, top), 1)
            result = jnp.zeros((tokens, top), F32)
            for k in range(top):
                own_value = jnp.sum(jnp.where(named_by[:, k : k + 1] == lane, partials, 0.0), axis=1, keepdims=True)
                result = jnp.where(place == k, own_value / probs_by[:, k : k + 1], result)
            token_unit = lax.broadcasted_iota(jnp.int32, (tokens, tokens), 0) == lax.broadcasted_iota(jnp.int32, (tokens, tokens), 1)
            prob_grad[...] = dot(result.astype(BF16), jnp.where(token_unit, 1.0, 0.0).astype(BF16), TN)

    for copy in info_copies:
        copy.wait_send()
    for w in range(waves):
        for offset in span:
            gather_copy(w, offset, via_of(w, offset)).wait_send()
        if plan[w][3]:
            swap(w).wait_send()
            served_rows = (half - 1) * per_dest
            if served_rows:
                arrived(send[w].at[pl.ds(0, served_rows)], send_sem.at[w])

            @pl.when(parity == 1)
            def _():
                arrived(send[w].at[pl.ds(0, per_dest)], send_sem.at[w])
        else:
            arrived(send[w].at[pl.ds(0, others)], send_sem.at[w])
    for v in range(returns):
        arrived(back_send[v].at[pl.ds(0, others)], back_send_sem.at[v])
        arrived(row_send[v].at[pl.ds(0, rows - 1)], row_send_sem.at[v])


def local(plan, back_plan, tokens, upstream, gate_probs, routes, w_gate, w_up, w_down):
    columns, rows = lax.axis_size("expert"), lax.axis_size("dp")
    count, width = tokens.shape
    top = routes.shape[1]
    units = w_gate.shape[2]
    experts = columns * rows // 2
    slots = columns * rows * (count * top // experts)
    waves, returns = len(plan), len(back_plan)
    wides = [wave[2] for wave in plan]
    backs = [wide + (experts if v == MARKED else 0) for v, (_, wide) in enumerate(back_plan)]
    dma = pltpu.SemaphoreType.DMA
    hbm, vmem = pl.BlockSpec(memory_space=pltpu.HBM), pl.BlockSpec(memory_space=pltpu.VMEM)
    input_grad, prob_grad, gate_grad, up_grad, down_grad = pl.pallas_call(
        functools.partial(kernel, (columns, rows, count, width, experts, units, top), plan, back_plan),
        out_shape=[
            pltpu.VMEM((count, width), BF16),
            pltpu.VMEM((top, count), F32),
            pltpu.VMEM(w_gate.shape, BF16),
            pltpu.VMEM(w_up.shape, BF16),
            pltpu.VMEM(w_down.shape, BF16),
        ],
        in_specs=[hbm] * 7,
        out_specs=[vmem] * 5,
        scratch_shapes=[
            pltpu.VMEM((rows, 2 * count, experts), BF16),
            pltpu.VMEM((slots, rows * count), BF16),
            pltpu.VMEM((slots, rows * count), BF16),
            pltpu.VMEM((rows * count, slots), BF16),
            pltpu.VMEM((width, 2 * units), BF16),
            pltpu.VMEM((units, width), BF16),
            pltpu.VMEM((slots, 2 * units), F32),
            pltpu.VMEM((slots, units), F32),
            pltpu.VMEM((slots, units), BF16),
            pltpu.VMEM((slots, 2 * units), BF16),
            pltpu.VMEM((count, top), F32),
            pltpu.VMEM((top, count), BF16),
            pltpu.VMEM((top, count), jnp.int32),
        ]
        + [pltpu.VMEM((rows, count, wide), BF16) for wide in wides]
        + [pltpu.VMEM((slots, wide), BF16) for wide in wides] * 2
        + [pltpu.VMEM((slots, wide), BF16) for wide in backs] * 2
        + [pltpu.VMEM((rows, count, wide), BF16) for wide in backs] * 2
        + [
            dma((waves,)),
            dma((5,)),
            dma((waves, rows)),
            dma((waves, rows)),
            dma((rows,)),
            dma((rows,)),
            dma((waves,)),
            dma((waves,)),
            dma((waves,)),
            dma((waves,)),
            dma((returns,)),
            dma((returns,)),
            dma((returns,)),
            dma((returns,)),
        ],
        compiler_params=pltpu.CompilerParams(
            collective_id=0, has_side_effects=True, vmem_limit_bytes=48 * 1024 * 1024
        ),
        cost_estimate=pl.CostEstimate(
            flops=16 * slots * width * units, bytes_accessed=24 * width * units, transcendentals=slots * units
        ),
    )(tokens, upstream, gate_probs.T, routes.T, w_gate, w_up, w_down)
    return input_grad, prob_grad.T, gate_grad, up_grad, down_grad


PLAN = (
    (0, 0, 1, 0, 0, 1),
    (0, 1, 1, 0, 0, 2),
    (0, 2, 2, 0, 0, 2),
    (0, 4, 2, 1, 0, 2),
    (0, 6, 2, 1, 1, 2),
    (1, 0, 2, 1, 1, 4),
    (1, 2, 2, 0, 2, 4),
    (1, 4, 2, 0, 3, 4),
    (1, 6, 2, 0, 4, 4),
)
PACE, SWAP_LAG = 3, 2
BACK_PLAN = tuple((start, 1) for start in range(8))
MARKED = 1
WINDOW = 4


def solution(mesh):
    both = ("expert", "dp")
    flat, deep = P(both, None), P(both, None, None)

    def whole(tokens, *others):
        unit = tokens.shape[1] // 8
        plan = tuple((kind, start * unit, wide * unit, bool(split), *rest) for kind, start, wide, split, *rest in PLAN)
        back_plan = tuple((start * unit, wide * unit) for start, wide in BACK_PLAN)
        return jax.shard_map(
            functools.partial(local, plan, back_plan),
            mesh=mesh,
            in_specs=(flat, flat, flat, flat, deep, deep, deep),
            out_specs=(flat, flat, deep, deep, deep),
            check_vma=False,
        )(tokens, *others)

    return whole
```

```python
import functools
import math

import jax
import jax.numpy as jnp
from jax import lax
from jax.experimental import pallas as pl
from jax.experimental.pallas import tpu as pltpu
from jax.sharding import PartitionSpec as P

MESH = pl.DeviceIdType.MESH
F32, BF16 = jnp.float32, jnp.bfloat16
NT = (((1,), (1,)), ((), ()))
TN = (((0,), (0,)), ((), ()))


def dot(a, b, dims=(((1,), (0,)), ((), ()))):
    return lax.dot_general(a, b, dims, preferred_element_type=F32)


def quotient(x, n):
    return x >> (n.bit_length() - 1) if n & (n - 1) == 0 else x // n


def remainder(x, n):
    return x & (n - 1) if n & (n - 1) == 0 else lax.rem(x, n)


def tiles(count, body):
    def step(i, carry):
        body(i)
        return carry

    lax.fori_loop(0, count, step, 0)


def kernel(sizes, plan, back_plan, *refs):
    columns, rows, tokens, width, experts, units, top = sizes
    waves, returns = len(plan), len(back_plan)
    refs = list(refs)

    def take(count):
        taken, refs[:count] = refs[:count], []
        return taken

    tok_hbm, ups_hbm, probs_hbm, routes_hbm, wg_hbm, wu_hbm, wd_hbm = take(7)
    input_grad, prob_grad, gate_out, up_out, down_out = take(5)
    info, pick, pick_scaled, merge, wgu, wd, acc, acc_back, hidden, delta, named_by, probs, routes = take(13)
    ring, send, recv = take(waves), take(waves), take(waves)
    back_send, back_recv, row_send, row_recv = take(returns), take(returns), take(returns), take(returns)
    own_sem, weight_sem, ring_send_sem, ring_recv_sem, info_send_sem, info_recv_sem = take(6)
    send_sem, recv_sem, swap_send_sem, swap_recv_sem = take(4)
    back_send_sem, back_recv_sem, row_send_sem, row_recv_sem = take(4)

    reach = tokens * top // experts
    per_dest = rows * reach
    slots = columns * per_dest
    half = columns // 2
    side = math.isqrt(half)
    me_c, me_r = lax.axis_index("expert"), lax.axis_index("dp")
    core, me_y, me_x = lax.rem(me_c, 2), lax.rem(me_c // 2, side), me_c // (2 * side)
    pair, parity = me_r // 2, lax.rem(me_r, 2)
    partner = me_r + 1 - 2 * parity

    def row_at(offset):
        return lax.rem(me_r + (offset % rows), rows)

    def place_at(i):
        return lax.rem(me_x + i // side, side) * side + lax.rem(me_y + lax.rem(i, side), side)

    def column_at(i):
        return place_at(i // 2) * 2 + lax.rem(core + lax.rem(i, 2), 2)

    def block(column):
        slot = lax.rem(column, 2) * half + column // 2
        return pl.ds(pl.multiple_of(slot * per_dest, per_dest), per_dest)

    def core_half(number):
        return pl.ds(pl.multiple_of(number * (half * per_dest), half * per_dest), half * per_dest)

    own = block(me_c)
    others = (columns - 1) * per_dest

    def arrived(buffer, sem):
        pltpu.make_async_copy(buffer, buffer, sem).wait()

    own_copies = []
    for w in range(waves):
        kind, start, wide = plan[w][:3]
        source = (tok_hbm, ups_hbm)[kind].at[:, pl.ds(start, wide)]
        copy = pltpu.make_async_copy(source, ring[w].at[me_r], own_sem.at[w])
        copy.start()
        own_copies.append(copy)
    route_copies = [
        pltpu.make_async_copy(probs_hbm, probs, weight_sem.at[3]),
        pltpu.make_async_copy(routes_hbm, routes, weight_sem.at[4]),
    ]
    for copy in route_copies:
        copy.start()
    weight_copies = [
        pltpu.make_async_copy(wg_hbm.at[0], wgu.at[:, pl.ds(0, units)], weight_sem.at[0]),
        pltpu.make_async_copy(wu_hbm.at[0], wgu.at[:, pl.ds(units, units)], weight_sem.at[1]),
        pltpu.make_async_copy(wd_hbm.at[0], wd, weight_sem.at[2]),
    ]
    for copy in weight_copies:
        copy.start()

    barrier = pltpu.get_barrier_semaphore()

    def greet_column(i):
        pl.semaphore_signal(barrier, inc=1, device_id=(column_at(i + 1), me_r), device_id_type=MESH)

    tiles(columns - 1, greet_column)
    for offset in range(1, rows):
        pl.semaphore_signal(barrier, inc=1, device_id=(me_c, row_at(offset)), device_id_type=MESH)

    for copy in route_copies:
        copy.wait()

    lane = lax.broadcasted_iota(jnp.int32, (tokens, experts), 1)
    named = jnp.zeros((tokens, experts), F32)
    weight = jnp.zeros((tokens, experts), F32)
    unit = lax.broadcasted_iota(jnp.int32, (top, top), 0) == lax.broadcasted_iota(jnp.int32, (top, top), 1)
    unit = jnp.where(unit, 1.0, 0.0).astype(BF16)
    named_by[...] = dot(routes[...].astype(F32).astype(BF16), unit, TN)
    probs_by = dot(probs[...], unit, TN)
    lane = lane.astype(F32)
    for k in range(top):
        hit = named_by[:, k : k + 1] == lane
        named = jnp.where(hit, 1.0, named)
        weight = jnp.where(hit, probs_by[:, k : k + 1], weight)
    upto = lax.broadcasted_iota(jnp.int32, (tokens, tokens), 0) >= lax.broadcasted_iota(jnp.int32, (tokens, tokens), 1)
    upto = jnp.where(upto, 1.0, 0.0).astype(BF16)
    rank = named * dot(upto, named.astype(BF16))
    info[me_r, 0:tokens, :] = rank.astype(BF16)
    info[me_r, tokens : 2 * tokens, :] = weight.astype(BF16)

    pl.semaphore_wait(barrier, columns - 1 + rows - 1)

    info_copies = []
    for offset in range(1, rows):
        copy = pltpu.make_async_remote_copy(
            info.at[me_r], info.at[me_r], info_send_sem.at[offset], info_recv_sem.at[offset],
            device_id=(me_c, row_at(offset)), device_id_type=MESH,
        )
        copy.start()
        info_copies.append(copy)

    span = [k for k in range(-((rows - 1) // 2), rows // 2 + 1) if k]

    def via_of(w, offset):
        steps, way = plan[w][5], 1 if offset > 0 else -1
        if steps == 1 or abs(offset) <= (2 if steps == 2 else 1):
            return 0
        return 2 * way if steps == 2 else offset - way

    def stage_of(w, offset):
        via = via_of(w, offset)
        return 0 if via == 0 else stage_of(w, via) + 1

    def gather_copy(w, offset, via):
        sign = 1 if w % 2 == 0 else -1
        source = row_at(-sign * via)
        return pltpu.make_async_remote_copy(
            ring[w].at[source], ring[w].at[source], ring_send_sem.at[w, offset % rows], ring_recv_sem.at[w, offset % rows],
            device_id=(me_c, row_at(sign * (offset - via))), device_id_type=MESH,
        )

    def gather_arrived(w, offset):
        sign = 1 if w % 2 == 0 else -1
        source = row_at(-sign * offset)
        pltpu.make_async_remote_copy(
            ring[w].at[source], ring[w].at[source], ring_send_sem.at[w, offset % rows], ring_recv_sem.at[w, offset % rows],
            device_id=(me_c, row_at(sign * offset)), device_id_type=MESH,
        ).wait_recv()

    def make_picks():
        for offset in range(1, rows):
            source = row_at(-offset)
            pltpu.make_async_remote_copy(
                info.at[source], info.at[source], info_send_sem.at[offset], info_recv_sem.at[offset],
                device_id=(me_c, row_at(offset)), device_id_type=MESH,
            ).wait_recv()
        count = rows * tokens
        expert = lax.broadcasted_iota(jnp.int32, (experts, slots), 0)
        slot = quotient(lax.broadcasted_iota(jnp.int32, (experts, slots), 1), per_dest)
        column = remainder(slot, half) * 2 + quotient(slot, half)
        spread = jnp.where(expert == column * (rows // 2) + pair, 1.0, 0.0).astype(BF16)
        expert = lax.broadcasted_iota(jnp.int32, (slots, experts), 1)
        slot = quotient(lax.broadcasted_iota(jnp.int32, (slots, experts), 0), per_dest)
        column = remainder(slot, half) * 2 + quotient(slot, half)
        spread_t = jnp.where(expert == column * (rows // 2) + pair, 1.0, 0.0).astype(BF16)
        ranks_in = info[:, 0:tokens, :].reshape(count, experts)
        weights_in = info[:, tokens : 2 * tokens, :].reshape(count, experts)

        def matches(ranks, token, place):
            wanted = remainder(place, per_dest) - reach * quotient(token, tokens) + 1
            return (ranks > 0.5) & (ranks == wanted.astype(F32))

        shape = (slots, count)
        match = matches(
            dot(spread_t, ranks_in, NT), lax.broadcasted_iota(jnp.int32, shape, 1), lax.broadcasted_iota(jnp.int32, shape, 0)
        )
        pick[...] = jnp.where(match, 1.0, 0.0).astype(BF16)
        pick_scaled[...] = jnp.where(match, dot(spread_t, weights_in, NT), 0.0).astype(BF16)
        shape = (count, slots)
        match = matches(
            dot(ranks_in, spread), lax.broadcasted_iota(jnp.int32, shape, 0), lax.broadcasted_iota(jnp.int32, shape, 1)
        )
        merge[...] = jnp.where(match, 1.0, 0.0).astype(BF16)

    def tile_of(wide):
        return 256 if wide % 256 == 0 else 128

    def send_wave(w):
        kind, _, wide, split = plan[w][:4]
        chosen = pick if kind == 0 else pick_scaled
        tile = tile_of(wide)

        def one(i):
            at = pl.ds(pl.multiple_of(i * tile, tile), tile)
            send[w][:, at] = dot(chosen[...], ring[w][:, :, at].reshape(rows * tokens, tile)).astype(BF16)

        tiles(wide // tile, one)

        def ship(to):
            pltpu.make_async_remote_copy(
                send[w].at[block(to)], recv[w].at[own], send_sem.at[w], recv_sem.at[w],
                device_id=(to, me_r), device_id_type=MESH,
            ).start()

        if split:
            @pl.when(parity == 0)
            def _():
                pltpu.make_async_copy(send[w].at[own], recv[w].at[own], recv_sem.at[w]).start()

            def step(i, carry):
                ship(place_at(lax.rem(i * 5, half)) * 2 + lax.rem(core + parity, 2))
                return carry

            lax.fori_loop(1 - parity, half, step, 0)
        else:
            recv[w][own, :] = send[w][own, :]
            tiles(columns - 1, lambda i: ship(column_at(lax.rem((i + 1) * 11, columns))))

    served = lax.rem(core + parity, 2)

    def swap(w):
        return pltpu.make_async_remote_copy(
            recv[w].at[core_half(served)], recv[w].at[core_half(served)], swap_send_sem.at[w], swap_recv_sem.at[w],
            device_id=(me_c, partner), device_id_type=MESH,
        )

    unit_tile = tile_of(2 * units)
    back_tile = 128
    block_rows = 64
    swapping, projected = [], []

    def project(w):
        kind, start, wide = plan[w][:3]
        opens = all(plan[v][0] != kind for v in projected)

        def forward(i):
            at = pl.ds(pl.multiple_of(i * unit_tile, unit_tile), unit_tile)
            value = dot(recv[w][...], wgu[start : start + wide, at])
            acc[:, at] = value if opens else acc[:, at] + value

        def backward(i):
            at = pl.ds(pl.multiple_of(i * back_tile, back_tile), back_tile)
            value = dot(recv[w][...], wd[at, start : start + wide], NT)
            acc_back[:, at] = value if opens else acc_back[:, at] + value

        if kind == 0:
            tiles(2 * units // unit_tile, forward)
        else:
            tiles(units // back_tile, backward)

    def activate(i):
        at = pl.ds(pl.multiple_of(i * block_rows, block_rows), block_rows)
        gate, up = acc[at, 0:units], acc[at, units : 2 * units]
        sigmoid = jax.nn.sigmoid(gate)
        activation = gate * sigmoid
        hidden[at, :] = (activation * up).astype(BF16)
        acc[at, 0:units] = up * (sigmoid * (1.0 + gate * (1.0 - sigmoid)))
        acc[at, units : 2 * units] = activation

    def finish(w):
        if plan[w][3]:
            swap(w).wait_recv()
        project(w)
        projected.append(w)
        if plan[w][0] == 0 and all(v in projected for v in range(waves) if plan[v][0] == 0):
            tiles(slots // block_rows, activate)

    started = [start for *_, start, _ in plan]
    heard = set()

    def hear(w, offset):
        if (w, offset) not in heard:
            heard.add((w, offset))
            gather_arrived(w, offset)

    farthest = sorted(span, key=lambda k: -abs(k))
    for tick in range(waves + PACE):
        for w in range(waves):
            for stage in range(rows):
                if tick != min(w, started[w] + stage):
                    continue
                if stage == 0:
                    own_copies[w].wait()
                for offset in farthest:
                    if stage_of(w, offset) == stage:
                        via = via_of(w, offset)
                        if via:
                            hear(w, via)
                        gather_copy(w, offset, via).start()
        if tick == 0:
            make_picks()
        if tick < waves:
            for offset in span:
                hear(tick, offset)
        landed = tick - PACE
        if landed == 0:
            for copy in weight_copies:
                copy.wait()
        if landed >= 0:
            if plan[landed][3]:
                arrived(recv[landed].at[core_half(served)], recv_sem.at[landed])
                swap(landed).start()
                swapping.append(landed)
            else:
                arrived(recv[landed].at[pl.ds(0, others)], recv_sem.at[landed])
        if tick < waves:
            send_wave(tick)
        if landed >= 0 and not plan[landed][3]:
            finish(landed)
        while swapping and (swapping[0] <= landed - SWAP_LAG or landed == waves - 1):
            finish(swapping.pop(0))

    own_expert = me_c * (rows // 2) + pair

    def deltas(i):
        at = pl.ds(pl.multiple_of(i * block_rows, block_rows), block_rows)
        back = acc_back[at, :]
        delta[at, 0:units] = (back * acc[at, 0:units]).astype(BF16)
        delta[at, units : 2 * units] = (back * acc[at, units : 2 * units]).astype(BF16)
        partial = jnp.sum(hidden[at, :].astype(F32) * back, axis=1, keepdims=True)
        place = lax.broadcasted_iota(jnp.int32, (block_rows, experts), 1)
        mark = back_plan[MARKED][1]
        back_send[MARKED][at, mark : mark + experts] = jnp.where(place == own_expert, partial, 0.0).astype(BF16)

    tiles(slots // block_rows, deltas)

    def send_back(v):
        start, wide = back_plan[v]
        part_tile = tile_of(wide)

        def term(i):
            at = pl.ds(pl.multiple_of(i * part_tile, part_tile), part_tile)
            from_row = pl.ds(pl.multiple_of(start + i * part_tile, part_tile), part_tile)
            back_send[v][:, at] = dot(delta[...], wgu[from_row, :], NT).astype(BF16)

        tiles(wide // part_tile, term)
        back_recv[v][own, :] = back_send[v][own, :]

        def ship_back(i):
            to = column_at(lax.rem((i + 1) * 11, columns))
            pltpu.make_async_remote_copy(
                back_send[v].at[block(to)], back_recv[v].at[own], back_send_sem.at[v], back_recv_sem.at[v],
                device_id=(to, me_r), device_id_type=MESH,
            ).start()

        tiles(columns - 1, ship_back)

    def weight_gradients(w):
        kind, start, wide = plan[w][:3]
        tile = tile_of(wide)

        def gate_up(i):
            at = pl.ds(pl.multiple_of(i * tile, tile), tile)
            to = pl.ds(pl.multiple_of(start + i * tile, tile), tile)
            value = dot(recv[w][:, at], delta[...], TN).astype(BF16)
            gate_out[0, to, :] = value[:, 0:units]
            up_out[0, to, :] = value[:, units : 2 * units]

        def down(i):
            at = pl.ds(pl.multiple_of(i * tile, tile), tile)
            to = pl.ds(pl.multiple_of(start + i * tile, tile), tile)
            down_out[0, :, to] = dot(hidden[...], recv[w][:, at], TN).astype(BF16)

        tiles(wide // tile, gate_up if kind == 0 else down)

    def combine(v):
        arrived(back_recv[v].at[pl.ds(0, others)], back_recv_sem.at[v])
        summed = dot(merge[...], back_recv[v][...]).astype(BF16).reshape(row_send[v].shape)
        row_send[v][...] = summed
        row_recv[v][me_r] = row_send[v][me_r]
        for offset in range(1, rows):
            to = row_at(offset)
            pltpu.make_async_remote_copy(
                row_send[v].at[to], row_recv[v].at[me_r], row_send_sem.at[v], row_recv_sem.at[v],
                device_id=(me_c, to), device_id_type=MESH,
            ).start()

    done = 0
    for v in range(min(WINDOW, returns)):
        send_back(v)
    for v in range(returns):
        while done < waves and done * returns <= (v + 1) * waves:
            weight_gradients(done)
            done = done + 1
        combine(v)
        if v + WINDOW < returns:
            send_back(v + WINDOW)

    for v in range(returns):
        start, wide = back_plan[v]
        arrived(row_recv[v].at[pl.ds(0, rows - 1)], row_recv_sem.at[v])
        total = row_recv[v][0].astype(F32)
        for r in range(1, rows):
            total = total + row_recv[v][r].astype(F32)
        input_grad[:, start : start + wide] = total[:, 0:wide].astype(BF16)
        if v == MARKED:
            partials = total[:, wide : wide + experts]
            place = lax.broadcasted_iota(jnp.int32, (tokens, top), 1)
            result = jnp.zeros((tokens, top), F32)
            for k in range(top):
                own_value = jnp.sum(jnp.where(named_by[:, k : k + 1] == lane, partials, 0.0), axis=1, keepdims=True)
                result = jnp.where(place == k, own_value / probs_by[:, k : k + 1], result)
            token_unit = lax.broadcasted_iota(jnp.int32, (tokens, tokens), 0) == lax.broadcasted_iota(jnp.int32, (tokens, tokens), 1)
            prob_grad[...] = dot(result.astype(BF16), jnp.where(token_unit, 1.0, 0.0).astype(BF16), TN)

    for copy in info_copies:
        copy.wait_send()
    for w in range(waves):
        for offset in span:
            gather_copy(w, offset, via_of(w, offset)).wait_send()
        if plan[w][3]:
            swap(w).wait_send()
            served_rows = (half - 1) * per_dest
            if served_rows:
                arrived(send[w].at[pl.ds(0, served_rows)], send_sem.at[w])

            @pl.when(parity == 1)
            def _():
                arrived(send[w].at[pl.ds(0, per_dest)], send_sem.at[w])
        else:
            arrived(send[w].at[pl.ds(0, others)], send_sem.at[w])
    for v in range(returns):
        arrived(back_send[v].at[pl.ds(0, others)], back_send_sem.at[v])
        arrived(row_send[v].at[pl.ds(0, rows - 1)], row_send_sem.at[v])


def local(plan, back_plan, tokens, upstream, gate_probs, routes, w_gate, w_up, w_down):
    columns, rows = lax.axis_size("expert"), lax.axis_size("dp")
    count, width = tokens.shape
    top = routes.shape[1]
    units = w_gate.shape[2]
    experts = columns * rows // 2
    slots = columns * rows * (count * top // experts)
    waves, returns = len(plan), len(back_plan)
    wides = [wave[2] for wave in plan]
    backs = [wide + (experts if v == MARKED else 0) for v, (_, wide) in enumerate(back_plan)]
    dma = pltpu.SemaphoreType.DMA
    hbm, vmem = pl.BlockSpec(memory_space=pltpu.HBM), pl.BlockSpec(memory_space=pltpu.VMEM)
    input_grad, prob_grad, gate_grad, up_grad, down_grad = pl.pallas_call(
        functools.partial(kernel, (columns, rows, count, width, experts, units, top), plan, back_plan),
        out_shape=[
            pltpu.VMEM((count, width), BF16),
            pltpu.VMEM((top, count), F32),
            pltpu.VMEM(w_gate.shape, BF16),
            pltpu.VMEM(w_up.shape, BF16),
            pltpu.VMEM(w_down.shape, BF16),
        ],
        in_specs=[hbm] * 7,
        out_specs=[vmem] * 5,
        scratch_shapes=[
            pltpu.VMEM((rows, 2 * count, experts), BF16),
            pltpu.VMEM((slots, rows * count), BF16),
            pltpu.VMEM((slots, rows * count), BF16),
            pltpu.VMEM((rows * count, slots), BF16),
            pltpu.VMEM((width, 2 * units), BF16),
            pltpu.VMEM((units, width), BF16),
            pltpu.VMEM((slots, 2 * units), F32),
            pltpu.VMEM((slots, units), F32),
            pltpu.VMEM((slots, units), BF16),
            pltpu.VMEM((slots, 2 * units), BF16),
            pltpu.VMEM((count, top), F32),
            pltpu.VMEM((top, count), BF16),
            pltpu.VMEM((top, count), jnp.int32),
        ]
        + [pltpu.VMEM((rows, count, wide), BF16) for wide in wides]
        + [pltpu.VMEM((slots, wide), BF16) for wide in wides] * 2
        + [pltpu.VMEM((slots, wide), BF16) for wide in backs] * 2
        + [pltpu.VMEM((rows, count, wide), BF16) for wide in backs] * 2
        + [
            dma((waves,)),
            dma((5,)),
            dma((waves, rows)),
            dma((waves, rows)),
            dma((rows,)),
            dma((rows,)),
            dma((waves,)),
            dma((waves,)),
            dma((waves,)),
            dma((waves,)),
            dma((returns,)),
            dma((returns,)),
            dma((returns,)),
            dma((returns,)),
        ],
        compiler_params=pltpu.CompilerParams(
            collective_id=0, has_side_effects=True, vmem_limit_bytes=58 * 1024 * 1024
        ),
        cost_estimate=pl.CostEstimate(
            flops=16 * slots * width * units, bytes_accessed=24 * width * units, transcendentals=slots * units
        ),
    )(tokens, upstream, gate_probs.T, routes.T, w_gate, w_up, w_down)
    return input_grad, prob_grad.T, gate_grad, up_grad, down_grad


PLAN = (
    (0, 0, 1, 0, 0, 1),
    (0, 1, 1, 0, 0, 2),
    (0, 2, 2, 0, 0, 2),
    (0, 4, 2, 1, 0, 2),
    (0, 6, 2, 1, 1, 2),
    (1, 0, 2, 1, 1, 4),
    (1, 2, 2, 0, 2, 4),
    (1, 4, 2, 0, 3, 4),
    (1, 6, 2, 0, 4, 4),
)
PACE, SWAP_LAG = 3, 2
BACK_PLAN = tuple((start, 1) for start in range(8))
MARKED = 1
WINDOW = 4


def solution(mesh):
    both = ("expert", "dp")
    flat, deep = P(both, None), P(both, None, None)

    def whole(tokens, *others):
        unit = tokens.shape[1] // 8
        plan = tuple((kind, start * unit, wide * unit, bool(split), *rest) for kind, start, wide, split, *rest in PLAN)
        back_plan = tuple((start * unit, wide * unit) for start, wide in BACK_PLAN)
        return jax.shard_map(
            functools.partial(local, plan, back_plan),
            mesh=mesh,
            in_specs=(flat, flat, flat, flat, deep, deep, deep),
            out_specs=(flat, flat, deep, deep, deep),
            check_vma=False,
        )(tokens, *others)

    return whole
```
